32 devices in a mesh: wide: 8 (over y, x, core), narrow: 4 (over z).
Axes of the slice: x: 2, y: 2, z: 4, core: 2. Of those that a mesh axis runs over, the one named last changes fastest.
Arguments:
- tokens: bfloat16 [16384, 1152], P(('wide', 'narrow')), may hold values from -6 to 6
- condition: bfloat16 [5, 1152], replicated, may hold values from -6 to 6
- q_weight: bfloat16 [1152, 1152], P(None, 'narrow'), may hold values from -0.1875 to 0.1875
- q_bias: bfloat16 [1152], P('narrow'), may hold values from -4 to 4
- k_weight: bfloat16 [1152, 1152], P(None, 'narrow'), may hold values from -0.1875 to 0.1875
- v_weight: bfloat16 [1152, 1152], P(None, 'narrow'), may hold values from -0.1875 to 0.1875
- v_bias: bfloat16 [1152], P('narrow'), may hold values from -4 to 4
- o_weight: bfloat16 [1152, 1152], P('narrow'), may hold values from -1.5 to 1.5
- o_bias: bfloat16 [1152], replicated, may hold values from -4 to 4
- up_weight: bfloat16 [1152, 4608], P(None, 'narrow'), may hold values from -0.1875 to 0.1875
- up_bias: bfloat16 [4608], P('narrow'), may hold values from -6 to 6
- down_weight: bfloat16 [4608, 1152], P('narrow'), may hold values from -0.09375 to 0.09375
- down_bias: bfloat16 [1152], replicated, may hold values from -4 to 4
- ada_weight: bfloat16 [1152, 6, 1152], P(None, None, 'narrow'), may hold values from -0.1875 to 0.1875
- ada_bias: bfloat16 [6, 1152], P(None, 'narrow'), may hold values from -6 to 6
- out_grad: bfloat16 [16384, 1152], P(('wide', 'narrow')), may hold values from -6 to 6
- slot_clip: int32 [16], P('wide'), may hold values from 0 to 4, as said below
- clip_patches: int32 [5], replicated, may hold values from 256 to 1024, as said below
Outputs:
- block_out: bfloat16 [16384, 1152], P(('wide', 'narrow'))
- grad_tokens: float32 [16384, 1152], P(('wide', 'narrow'))
- grad_condition: float32 [5, 1152], replicated
- grad_q_weight: float32 [1152, 1152], P(None, 'narrow')
- grad_q_bias: float32 [1152], P('narrow')
- grad_k_weight: float32 [1152, 1152], P(None, 'narrow')
- grad_v_weight: float32 [1152, 1152], P(None, 'narrow')
- grad_v_bias: float32 [1152], P('narrow')
- grad_o_weight: float32 [1152, 1152], P('narrow')
- grad_o_bias: float32 [1152], replicated
- grad_up_weight: float32 [1152, 4608], P(None, 'narrow')
- grad_up_bias: float32 [4608], P('narrow')
- grad_down_weight: float32 [4608, 1152], P('narrow')
- grad_down_bias: float32 [1152], replicated
- grad_ada_weight: float32 [1152, 6, 1152], P(None, None, 'narrow')
- grad_ada_bias: float32 [6, 1152], P(None, 'narrow')
The draws below stay inside these ranges and needn't reach their ends.
Inputs may be any that keep to these rules, and one draw needn't show every extreme that they name: Slot s holds rows s * 1024 to (s + 1) * 1024 - 1 of tokens, filled with whole frames of clip slot_clip[s]. Every clip fills some slot, and the first and the last slot belong to the same clip. `clip_patches`: each clip has frames of 256 or of 1024 patches; both occur.
All inputs are finite; a program needn't handle non-finite values.
Results may differ from the reference program's by a relative error of at most 0.013.
The reference program's roundings to bfloat16 on the way count: a program that leaves them out, or rounds other values in their place, can miss the bound.
Values may be sent and summed in bfloat16 or wider, within the bound.
No kernel may reach another device: no remote copies, remote signals or barrier semaphores. Data moves between devices by JAX's collectives and lax.ppermute only.
A program may use at most 320 MiB of HBM per device.

```python
import jax
import jax.numpy as jnp
from jax import lax

D = 1152
HEADS = 16
HDIM = 72
FF = 4608
CLIPS = 5
PATCH_HI = 1024
PATCH_LO = 256
TOK_DEV = 2048
SLOTS = 2
SLOTS_ALL = 16
TOKENS = 16384
N_WIDE = 8


def draw_slot_clip(key, part):
    key = jax.random.fold_in(key, 11)
    key_base, key_ends, key_order = jax.random.split(key, 3)
    base = jax.random.randint(key_base, (SLOTS_ALL,), 0, CLIPS, dtype=jnp.int32)
    end_clip = jax.random.randint(key_ends, (), 0, CLIPS, dtype=jnp.int32)
    order = jax.random.permutation(key_order, SLOTS_ALL - 2) + 1
    base = base.at[order[:CLIPS]].set(jnp.arange(CLIPS, dtype=jnp.int32))
    base = base.at[0].set(end_clip)
    base = base.at[SLOTS_ALL - 1].set(end_clip)
    return base.astype(jnp.int32)


def draw_clip_patches(key, part):
    key = jax.random.fold_in(key, 12)
    key_bits, key_order = jax.random.split(key)
    picks = jax.random.randint(key_bits, (CLIPS,), 0, 2, dtype=jnp.int32)
    order = jax.random.permutation(key_order, CLIPS)
    picks = picks.at[order[0]].set(1)
    picks = picks.at[order[1]].set(0)
    return jnp.where(picks == 1, PATCH_HI, PATCH_LO).astype(jnp.int32)


def steps_of(stream_key, extent, shards, smallest, largest):
    factor_of, own = 1.0, jax.random.fold_in(stream_key, 6)
    for axis_at, blocks in shards:
        draws = jnp.exp(jax.random.uniform(jax.random.fold_in(own, axis_at), (blocks,), jnp.float32, smallest / len(shards), largest / len(shards)))
        factor_of = factor_of * jnp.repeat(draws, extent[axis_at] // blocks).reshape([-1 if axis == axis_at else 1 for axis in range(len(extent))])
    return factor_of


def bell_draw(rng, dims, scale, most, cuts=(), held_as=jnp.bfloat16):
    values = jax.random.normal(rng, dims, jnp.float32) * scale
    if len(cuts) > 0:
        values = steps_of(rng, dims, cuts, -0.22, 0.18) * values
    return jnp.clip(values, min=-most, max=most).astype(held_as)


def setup_inputs(seed: int = 0) -> dict:
    streams_of = jax.random.split(jax.random.key(seed), 19)
    tokens = bell_draw(streams_of[0], (TOKENS, D), 1.0, 6.0, ((0, 32),))
    condition = bell_draw(streams_of[1], (CLIPS, D), 1.0, 6.0)
    q_weight = bell_draw(streams_of[2], (D, D), D ** -0.5, 0.1875, ((1, 4),))
    q_bias = bell_draw(streams_of[3], (D,), 0.3, 4.0, ((0, 4),))
    k_weight = bell_draw(streams_of[4], (D, D), D ** -0.5, 0.1875, ((1, 4),))
    v_weight = bell_draw(streams_of[5], (D, D), D ** -0.5, 0.1875, ((1, 4),))
    v_bias = bell_draw(streams_of[6], (D,), 0.3, 4.0, ((0, 4),))
    o_weight = bell_draw(streams_of[7], (D, D), (max(D // 64, 4)) ** -0.5, 1.5, ((0, 4),))
    o_bias = bell_draw(streams_of[8], (D,), 0.3, 4.0)
    up_weight = bell_draw(streams_of[9], (D, FF), D ** -0.5, 0.1875, ((1, 4),))
    up_bias = bell_draw(streams_of[10], (FF,), 0.5, 6.0, ((0, 4),))
    down_weight = bell_draw(streams_of[11], (FF, D), FF ** -0.5, 0.09375, ((0, 4),))
    down_bias = bell_draw(streams_of[12], (D,), 0.3, 4.0)
    ada_weight = bell_draw(streams_of[13], (D, 6, D), D ** -0.5, 0.1875, ((2, 4),))
    ada_bias = bell_draw(streams_of[14], (6, D), 0.5, 6.0, ((1, 4),))
    out_grad = bell_draw(streams_of[15], (TOKENS, D), 1.0, 6.0, ((0, 32),))
    slot_clip = draw_slot_clip(jax.random.fold_in(streams_of[18], 71), 0)
    clip_patches = draw_clip_patches(jax.random.fold_in(streams_of[18], 71), 0)
    return dict(tokens=tokens, condition=condition, q_weight=q_weight, q_bias=q_bias, k_weight=k_weight, v_weight=v_weight, v_bias=v_bias, o_weight=o_weight, o_bias=o_bias, up_weight=up_weight, up_bias=up_bias, down_weight=down_weight, down_bias=down_bias, ada_weight=ada_weight, ada_bias=ada_bias, out_grad=out_grad, slot_clip=slot_clip, clip_patches=clip_patches)


@jax.custom_vjp
def low(v):
    return lax.optimization_barrier(v.astype(jnp.bfloat16)).astype(jnp.float32)

@jax.custom_vjp
def low_back(v):
    return v

def low_keep(v):
    return (low(v), None)

def low_pass(kept, grad):
    return (grad,)

def back_keep(v):
    return (v, None)

def back_low(kept, grad):
    return (low(grad),)
low.defvjp(low_keep, low_pass)
low_back.defvjp(back_keep, back_low)
epsilon = 1e-06
masked_score = -1000000000.0
highest = lax.Precision.HIGHEST

def normalize(row_block):
    centred = row_block - lax.optimization_barrier(jnp.mean(row_block, axis=-1, keepdims=True))
    variance = lax.optimization_barrier(jnp.mean(centred * centred, axis=-1, keepdims=True))
    return centred * lax.rsqrt(variance + epsilon)

def frame_attention(operands):
    q_slot, k_slot, v_slot, patches = operands
    position = jnp.arange(PATCH_HI, dtype=jnp.int32)
    frame_id = position // patches
    same_frame = frame_id[:, None] == frame_id[None, :]
    scores = jnp.einsum('qhd,khd->hqk', q_slot, k_slot, precision=highest) * HDIM ** (-0.5)
    scores = low_back(scores)
    scores = jnp.where(same_frame[None], scores, masked_score)
    attn_weights = low(jax.nn.softmax(scores, axis=-1))
    return jnp.einsum('hqk,khd->qhd', attn_weights, v_slot, precision=highest)

def group_forward(params, modulation, group_rows, group_slots, clip_patches):
    q_weight, q_bias, k_weight, v_weight, v_bias, o_weight, o_bias, up_weight, up_bias, down_weight, down_bias = params
    row_slot = jnp.arange(TOK_DEV, dtype=jnp.int32) // PATCH_HI
    row_clip = group_slots[row_slot]
    one_hot = (row_clip[:, None] == jnp.arange(CLIPS, dtype=jnp.int32)[None, :]).astype(modulation.dtype)
    row_mod = jnp.dot(one_hot, modulation.reshape(CLIPS, 6 * D), precision=highest).reshape(TOK_DEV, 6, D)
    attn_in = low(normalize(group_rows) * (1.0 + row_mod[:, 1]) + row_mod[:, 0])
    q_rows = low(low_back(jnp.dot(attn_in, q_weight, precision=highest) + q_bias))
    k_rows = low(low_back(jnp.dot(attn_in, k_weight, precision=highest)))
    v_rows = low(low_back(jnp.dot(attn_in, v_weight, precision=highest) + v_bias))
    slot_shape = (SLOTS, PATCH_HI, HEADS, HDIM)
    slot_patches = clip_patches[group_slots]
    attended = lax.map(jax.checkpoint(frame_attention), (q_rows.reshape(slot_shape), k_rows.reshape(slot_shape), v_rows.reshape(slot_shape), slot_patches))
    attended = low(low_back(attended.reshape(TOK_DEV, D)))
    branch_one = low_back(jnp.dot(attended, o_weight, precision=highest) + o_bias)
    middle = group_rows + row_mod[:, 2] * branch_one
    mlp_in = low(normalize(middle) * (1.0 + row_mod[:, 4]) + row_mod[:, 3])
    pre_act = low_back(jnp.dot(mlp_in, up_weight, precision=highest) + up_bias)
    hidden = low(jax.nn.gelu(pre_act, approximate=True))
    branch_two = low_back(jnp.dot(hidden, down_weight, precision=highest) + down_bias)
    return middle + row_mod[:, 5] * branch_two

def forward(tokens, condition, params, ada_matrix, ada_shift, slot_clip, clip_patches):
    silu_cond = low(jax.nn.silu(condition))
    modulation = jnp.einsum('cd,dke->cke', silu_cond, ada_matrix, precision=highest) + ada_shift
    groups = tokens.reshape(N_WIDE, TOK_DEV, D)
    group_slots = slot_clip.reshape(N_WIDE, SLOTS)

    def one_group(operands):
        return group_forward(params, modulation, operands[0], operands[1], clip_patches)
    outputs = lax.map(jax.checkpoint(one_group), (groups, group_slots))
    return outputs.reshape(TOKENS, D)

def to_float(array):
    return array.astype(jnp.float32)

def reference(tokens, condition, q_weight, q_bias, k_weight, v_weight, v_bias, o_weight, o_bias, up_weight, up_bias, down_weight, down_bias, ada_weight, ada_bias, out_grad, slot_clip, clip_patches):
    params = tuple((to_float(weight_array) for weight_array in (q_weight, q_bias, k_weight, v_weight, v_bias, o_weight, o_bias, up_weight, up_bias, down_weight, down_bias)))

    def apply_block(tok_rows, cond_rows, block_params, ada_matrix, ada_shift):
        return forward(tok_rows, cond_rows, block_params, ada_matrix, ada_shift, slot_clip, clip_patches)
    block_out, pullback = jax.vjp(apply_block, to_float(tokens), to_float(condition), params, to_float(ada_weight), to_float(ada_bias))
    grad_tok, grad_cond, grad_params, grad_ada_matrix, grad_ada_shift = pullback(to_float(out_grad))
    return (block_out.astype(jnp.bfloat16), grad_tok, grad_cond, grad_params[0], grad_params[1], grad_params[2], grad_params[3], grad_params[4], grad_params[5], grad_params[6], grad_params[7], grad_params[8], grad_params[9], grad_params[10], grad_ada_matrix, grad_ada_shift)
```

```python
import functools

import jax
import jax.numpy as jnp
from jax import lax
from jax.experimental import pallas as pl
from jax.experimental.pallas import tpu as pltpu
from jax.sharding import PartitionSpec as P

HDIM = 72
PATCH_HI = 1024
BLOCK = 256
ROW_BLOCK = 256
HIDDEN_BLOCK = 384
VMEM_LIMIT = 48 * 1024 * 1024

epsilon = 1e-06
highest = lax.Precision.HIGHEST
EXP2_SCALE = HDIM ** (-0.5) * 1.4426950408889634
f32 = jnp.float32
bf16 = jnp.bfloat16


def normalize(row_block):
    centred = row_block - jnp.mean(row_block, axis=-1, keepdims=True)
    variance = jnp.mean(centred * centred, axis=-1, keepdims=True)
    inverse = lax.rsqrt(variance + epsilon)
    return (centred * inverse, inverse)


def norm_back(d_normed, normed, inverse):
    first_mean = jnp.mean(d_normed, axis=-1, keepdims=True)
    second_mean = jnp.mean(d_normed * normed, axis=-1, keepdims=True)
    return inverse * (d_normed - first_mean - normed * second_mean)


def gelu_and_slope(values):
    root = (2.0 / jnp.pi) ** 0.5
    square = values * values
    tanh = jnp.tanh(root * (values + 0.044715 * (square * values)))
    half = 0.5 * (1.0 + tanh)
    slope = half + 0.5 * values * (1.0 - tanh * tanh) * (root + (3 * 0.044715 * root) * square)
    return values * half, slope


def dot(left, right):
    return jnp.dot(left, right, preferred_element_type=f32)


def dot_t(left, right):
    return lax.dot_general(left, right, (((1,), (1,)), ((), ())), preferred_element_type=f32)


def contract_rows(left, right):
    return lax.dot_general(left, right, (((0,), (0,)), ((), ())), preferred_element_type=f32)


def left_t_right_t(left, right):
    return lax.dot_general(left, right, (((0,), (1,)), ((), ())), preferred_element_type=f32)


def kernel_call(kernel, outs, **options):
    return pl.pallas_call(
        kernel,
        out_shape=outs,
        compiler_params=pltpu.CompilerParams(vmem_limit_bytes=VMEM_LIMIT),
        cost_estimate=pl.CostEstimate(flops=0, bytes_accessed=1024, transcendentals=0),
        **options,
    )


def whole(array):
    return pl.BlockSpec(array.shape, lambda *_: (0,) * len(array.shape))


def row_call(body, rows_in, vectors, out_types, term_count=0):
    rows, width = rows_in[0].shape[0], vectors[0].shape[1]
    step_rows = min(ROW_BLOCK, rows)
    rows_in = [each if isinstance(each, tuple) else (each, 0) for each in rows_in]

    def kernel(*refs):
        row_refs = refs[: len(rows_in)]
        vector_refs = refs[len(rows_in) : len(rows_in) + len(vectors)]
        out_refs = refs[len(rows_in) + len(vectors) :]
        outs, terms = body([ref[...] for ref in row_refs], vector_refs)
        for ref, out in zip(out_refs, outs):
            ref[...] = out.astype(ref.dtype)
        if term_count:
            sums_ref = refs[-1]

            @pl.when(pl.program_id(0) == 0)
            def _():
                sums_ref[...] = jnp.zeros_like(sums_ref)

            for index, term in enumerate(terms):
                sums_ref[index : index + 1, :] += jnp.sum(term, axis=0, keepdims=True)

    outs = [jax.ShapeDtypeStruct((rows, width), kind) for kind in out_types]
    out_specs = [pl.BlockSpec((step_rows, width), lambda index: (index, 0))] * len(outs)
    if term_count:
        outs.append(jax.ShapeDtypeStruct((8, width), f32))
        out_specs.append(pl.BlockSpec((8, width), lambda index: (0, 0)))
    return kernel_call(
        kernel,
        outs,
        grid=(rows // step_rows,),
        in_specs=[
            pl.BlockSpec((step_rows, each.shape[1]), lambda index, first=first: (first // step_rows + index, 0))
            for each, first in rows_in
        ]
        + [whole(each) for each in vectors],
        out_specs=out_specs,
    )(*(each for each, _ in rows_in), *vectors)


def modulated_rows_kernel(row_count, *refs):
    mod_ref, out_ref = refs[-2:]
    for index, ref in enumerate(refs[:row_count]):
        normed = normalize(ref[...].astype(f32))[0]
        out_ref[index] = (normed * (1.0 + mod_ref[1:2, :]) + mod_ref[0:1, :]).astype(bf16)


def modulated_rows(row_blocks, modulation):
    rows, width = row_blocks[0].shape
    count = len(row_blocks)
    out = kernel_call(
        functools.partial(modulated_rows_kernel, count),
        jax.ShapeDtypeStruct((count, rows, width), bf16),
        grid=(rows // ROW_BLOCK,),
        in_specs=[pl.BlockSpec((ROW_BLOCK, width), lambda index: (index, 0))] * count
        + [whole(modulation)],
        out_specs=pl.BlockSpec((count, ROW_BLOCK, width), lambda index: (0, index, 0)),
    )(*row_blocks, modulation)
    return out.reshape(count * rows, width)


def qkv_kernel(rows_ref, pack_ref, bias_ref, out_ref):
    columns = out_ref.shape[1]
    rows = dot_t(rows_ref[...], pack_ref[:columns]) + bias_ref[...].astype(f32)
    out_ref[...] = rows.astype(bf16)


def qkv_rows(rows, pack, bias):
    columns = pack.shape[0] // 4 * 3
    bias = bias.reshape(1, columns)
    return kernel_call(
        qkv_kernel,
        jax.ShapeDtypeStruct((rows.shape[0], columns), bf16),
        grid=(rows.shape[0] // BLOCK,),
        in_specs=[
            pl.BlockSpec((BLOCK, rows.shape[1]), lambda index: (index, 0)),
            whole(pack),
            whole(bias),
        ],
        out_specs=pl.BlockSpec((BLOCK, columns), lambda index: (index, 0)),
    )(rows, pack, bias)


def frame_loop(patches_ref, rows, heads, stages):
    is_full = patches_ref[0] == PATCH_HI
    first, second, third = stages

    def run(full):
        units = [(block * BLOCK, head) for block in range(rows // BLOCK) for head in range(heads)]
        begun = first(*units[0], full)
        done = None
        for at, unit in enumerate(units):
            coming = first(*units[at + 1], full) if at + 1 < len(units) else None
            if done is not None:
                third(*units[at - 1], full, done)
            done = second(*unit, full, begun)
            begun = coming
        third(*units[-1], full, done)

    @pl.when(is_full)
    def _():
        run(True)

    @pl.when(jnp.logical_not(is_full))
    def _():
        run(False)


def attention_forward_kernel(
    first_row, patches_ref, qkv_ref, attended_ref, turned_ref, lse_ref, out_scratch
):
    heads = qkv_ref.shape[1] // (3 * HDIM)

    def columns(start, full, part, head):
        at = (part * heads + head) * HDIM
        rows = slice(0, PATCH_HI) if full else slice(first_row + start, first_row + start + BLOCK)
        return qkv_ref[rows, at : at + HDIM]

    def scores(start, head, full):
        return dot_t(columns(start, full, 1, head), columns(start, False, 0, head))

    def softmax(start, head, full, logits):
        out_rows = slice(start, start + BLOCK)
        top = jnp.max(logits, axis=0, keepdims=True) * EXP2_SCALE
        exp_scores = jnp.exp2(logits * EXP2_SCALE - top)
        total = jnp.sum(exp_scores, axis=0, keepdims=True)
        lse_ref[head : head + 1, out_rows] = top + jnp.log2(total)
        return (exp_scores * (1.0 / total)).astype(bf16)

    def values(start, head, full, weights):
        out_scratch[head * HDIM : (head + 1) * HDIM, start : start + BLOCK] = contract_rows(
            columns(start, full, 2, head), weights
        )

    frame_loop(patches_ref, lse_ref.shape[1], heads, (scores, softmax, values))
    attended_ref[...] = out_scratch[...].T.astype(bf16)
    turned_ref[...] = out_scratch[...].astype(bf16)


VMEM_SPEC = pl.BlockSpec(memory_space=pltpu.VMEM)
SMEM_SPEC = pl.BlockSpec(memory_space=pltpu.SMEM)


def attention_forward(qkv, patches, first_row, rows):
    width = qkv.shape[1] // 3
    return kernel_call(
        functools.partial(attention_forward_kernel, first_row),
        (
            jax.ShapeDtypeStruct((rows, width), bf16),
            jax.ShapeDtypeStruct((width, rows), bf16),
            jax.ShapeDtypeStruct((width // HDIM, rows), f32),
        ),
        in_specs=[SMEM_SPEC, VMEM_SPEC],
        out_specs=(VMEM_SPEC, VMEM_SPEC, VMEM_SPEC),
        scratch_shapes=[pltpu.VMEM((width, rows), f32)],
    )(patches, qkv)


def attention_backward_kernel(first_row, first, last, *refs):
    patches_ref, qkv_ref, d_rows_ref, pack_ref, lse_ref = refs[:5]
    sums_ref = refs[5] if not first else None
    d_query_ref, d_query_turned_ref, d_kv_ref, *rest = refs[5 if first else 6 :]
    d_kv_turned_ref = rest[0] if last else None
    query_scratch, kv_scratch, d_scratch = rest[-3:]
    local = d_query_ref.shape[1]
    heads = local // HDIM
    scale = HDIM ** (-0.5)
    kv_scratch[...] = jnp.zeros_like(kv_scratch) if first else sums_ref[...]
    d_scratch[...] = dot_t(d_rows_ref[...], pack_ref[3 * local :]).astype(bf16)

    def columns(start, full, part, head):
        at = (part * heads + head) * HDIM
        rows = slice(0, PATCH_HI) if full else slice(first_row + start, first_row + start + BLOCK)
        return qkv_ref[rows, at : at + HDIM]

    def d_out(start, head):
        return d_scratch[start : start + BLOCK, head * HDIM : (head + 1) * HDIM]

    def products(start, head, full):
        logits = dot_t(columns(start, full, 1, head), columns(start, False, 0, head))
        return logits, dot_t(columns(start, full, 2, head), d_out(start, head))

    def d_softmax(start, head, full, pair):
        logits, d_weights = pair
        probs = jnp.exp2(logits * EXP2_SCALE - lse_ref[head : head + 1, start : start + BLOCK])
        delta = jnp.sum(probs * d_weights, axis=0, keepdims=True)
        return probs.astype(bf16), (probs * (d_weights - delta)).astype(bf16)

    def gradients(start, head, full, pair):
        probs, d_scores = pair
        at = slice(head * HDIM, (head + 1) * HDIM)
        v_at = slice(local + head * HDIM, local + (head + 1) * HDIM)
        k_rows = slice(0, PATCH_HI) if full else slice(first_row + start, first_row + start + BLOCK)
        query_scratch[at, start : start + BLOCK] = (
            contract_rows(columns(start, full, 1, head), d_scores) * scale
        )
        kv_scratch[at, k_rows] += left_t_right_t(columns(start, False, 0, head), d_scores) * scale
        kv_scratch[v_at, k_rows] += left_t_right_t(d_out(start, head), probs)

    frame_loop(patches_ref, lse_ref.shape[1], heads, (products, d_softmax, gradients))
    d_query_ref[...] = query_scratch[...].T.astype(bf16)
    d_query_turned_ref[...] = query_scratch[...].astype(bf16)
    if last:
        d_kv_ref[...] = kv_scratch[...].T.astype(bf16)
        d_kv_turned_ref[...] = kv_scratch[...].astype(bf16)
    else:
        d_kv_ref[...] = kv_scratch[...]


def attention_backward(qkv, d_rows, pack, lse, patches, sums, first_row, last):
    local = pack.shape[0] // 4
    rows = d_rows.shape[0]
    first = sums is None
    turned = (2 * local, PATCH_HI)
    extra = [] if first else [sums]
    outs = [jax.ShapeDtypeStruct((rows, local), bf16), jax.ShapeDtypeStruct((local, rows), bf16)]
    if last:
        outs += [jax.ShapeDtypeStruct(turned[::-1], bf16), jax.ShapeDtypeStruct(turned, bf16)]
    else:
        outs.append(jax.ShapeDtypeStruct(turned, f32))
    return kernel_call(
        functools.partial(attention_backward_kernel, first_row, first, last),
        outs,
        in_specs=[SMEM_SPEC] + [VMEM_SPEC] * (4 + len(extra)),
        out_specs=[VMEM_SPEC] * len(outs),
        scratch_shapes=[
            pltpu.VMEM((local, rows), f32),
            pltpu.VMEM(turned, f32),
            pltpu.VMEM((rows, local), bf16),
        ],
    )(patches, qkv, d_rows, pack, lse, *extra)


def feed_forward_kernel(last_types, shard_count, *refs):
    x_ref, grad_ref, mod_ref, bias_ref = refs[:4]
    up_refs = refs[4 : 4 + shard_count]
    down_refs = refs[4 + shard_count : 4 + 2 * shard_count]
    hidden_ref, d_pre_ref, d_branch_ref, d_mlp_ref, branch_ref, sums_ref = refs[-8:-2]
    d_mlp_scratch, branch_scratch = refs[-2:]

    @pl.when(pl.program_id(0) == 0)
    def _():
        d_mlp_scratch[...] = jnp.zeros_like(d_mlp_scratch)
        branch_scratch[...] = jnp.zeros_like(branch_scratch)
        d_branch_ref[...] = (mod_ref[5:6, :] * grad_ref[...].astype(f32)).astype(bf16)

    sums_ref[...] = jnp.zeros_like(sums_ref)
    rows = x_ref.shape[0]
    for start in range(0, rows, BLOCK):
        block = slice(start, start + BLOCK)
        d_mlp, branch = 0.0, 0.0
        for shard in range(shard_count):
            pre_act = dot(x_ref[block], up_refs[shard][...]) + bias_ref[shard].astype(f32)
            hidden, slope = gelu_and_slope(pre_act)
            d_pre = (dot_t(d_branch_ref[block], down_refs[shard][...]) * slope).astype(bf16)
            hidden = hidden.astype(bf16)
            hidden_ref[shard, block] = hidden
            d_pre_ref[shard, block] = d_pre
            sums_ref[shard : shard + 1] += jnp.sum(d_pre.astype(f32), axis=0, keepdims=True)
            d_mlp = d_mlp + dot_t(d_pre, up_refs[shard][...])
            branch = branch + dot(hidden, down_refs[shard][...])
        d_mlp_scratch[block] += d_mlp
        branch_scratch[block] += branch

    @pl.when(pl.program_id(0) == pl.num_programs(0) - 1)
    def _():
        d_mlp_ref[...] = d_mlp_scratch[...].astype(d_mlp_ref.dtype)
        branch_ref[...] = branch_scratch[...].astype(branch_ref.dtype)


def feed_forward(rows, grad, modulation, biases, ups, downs, sum_type):
    row_count, width = rows.shape
    shard_count = len(ups)
    hidden_local = biases.shape[-1]
    step = HIDDEN_BLOCK if hidden_local % HIDDEN_BLOCK == 0 else hidden_local
    in_specs = [whole(rows), whole(grad), whole(modulation)]
    in_specs.append(pl.BlockSpec((shard_count, 1, step), lambda index: (0, 0, index)))
    for _, first in ups:
        in_specs.append(pl.BlockSpec((width, step), lambda index, first=first: (0, first + index)))
    for _, first in downs:
        in_specs.append(pl.BlockSpec((step, width), lambda index, first=first: (index, first)))
    by_shard = pl.BlockSpec((shard_count, row_count, step), lambda index: (0, 0, index))
    flat = jax.ShapeDtypeStruct((row_count, width), sum_type)
    return kernel_call(
        functools.partial(feed_forward_kernel, sum_type, shard_count),
        [
            jax.ShapeDtypeStruct((shard_count, row_count, hidden_local), bf16),
            jax.ShapeDtypeStruct((shard_count, row_count, hidden_local), bf16),
            jax.ShapeDtypeStruct((row_count, width), bf16),
            flat,
            flat,
            jax.ShapeDtypeStruct((8, hidden_local), f32),
        ],
        grid=(hidden_local // step,),
        in_specs=in_specs,
        out_specs=[by_shard, by_shard]
        + [pl.BlockSpec((row_count, width), lambda index: (0, 0))] * 3
        + [pl.BlockSpec((8, step), lambda index: (0, index))],
        scratch_shapes=[pltpu.VMEM((row_count, width), f32)] * 2,
    )(rows, grad, modulation, biases, *(each for each, _ in ups), *(each for each, _ in downs))


def mlp_gradient_kernel(member_count, *refs):
    out_ref = refs[-1]
    is_up = pl.program_id(0) % 2 == 0
    pieces, _, rows, width = out_ref.shape

    def store(lefts, rights):
        total = sum(contract_rows(left, right) for left, right in zip(lefts, rights))
        out_ref[:, 0] = total.astype(bf16).reshape(pieces, rows, width)

    groups = [refs[at * member_count : (at + 1) * member_count] for at in range(4)]
    x_refs, d_branch_refs, hidden_refs, d_pre_refs = groups

    @pl.when(is_up)
    def _():
        store([ref[...] for ref in x_refs], [ref[0] for ref in d_pre_refs])

    @pl.when(jnp.logical_not(is_up))
    def _():
        store([ref[0] for ref in hidden_refs], [ref[...] for ref in d_branch_refs])


def mlp_gradients(x_rows, d_branch_rows, hidden, d_pre, pieces):
    shard_count, row_count, hidden_local = hidden[0].shape
    width = x_rows[0].shape[1]
    rows = hidden_local // pieces
    if hidden_local != width or rows % 16:
        parts = []
        for shard in range(shard_count):
            up = sum(contract_rows(left, right[shard]) for left, right in zip(x_rows, d_pre))
            down = sum(contract_rows(left[shard], right) for left, right in zip(hidden, d_branch_rows))
            parts += [up.reshape(pieces, rows, width), down.reshape(pieces, rows, width)]
        return jnp.stack(parts, axis=1).astype(bf16)
    by_shard = pl.BlockSpec((1, row_count, hidden_local), lambda index: (index // 2, 0, 0))
    return kernel_call(
        functools.partial(mlp_gradient_kernel, len(x_rows)),
        jax.ShapeDtypeStruct((pieces, 2 * shard_count, rows, width), bf16),
        grid=(2 * shard_count,),
        in_specs=[whole(each) for each in (*x_rows, *d_branch_rows)]
        + [by_shard] * (2 * len(x_rows)),
        out_specs=pl.BlockSpec((pieces, 1, rows, width), lambda index: (0, index, 0, 0)),
    )(*x_rows, *d_branch_rows, *hidden, *d_pre)


def attn_gradient_kernel(member_count, *refs):
    core_ref, in_ref, d_kv_ref = refs[:3]
    d_query_refs, d_branch_refs = refs[3 : 3 + member_count], refs[3 + member_count : 3 + 2 * member_count]
    attended_refs = refs[3 + 2 * member_count : -4]
    keep_ref, send_ref, sums_ref, out_ref = refs[-4:]
    local, rows = d_query_refs[0].shape
    query = sum(
        dot(ref[...], in_ref[at * rows : (at + 1) * rows]) for at, ref in enumerate(d_query_refs)
    )
    out_ref[:local] = query.astype(bf16)
    out_ref[local : 3 * local] = dot(d_kv_ref[...], in_ref[...]).astype(bf16)
    start, out = 0, 0.0
    for ref in attended_refs:
        first = start % rows
        out = out + dot(ref[...], d_branch_refs[start // rows][first : first + ref.shape[1]])
        start += ref.shape[1]
    out_ref[3 * local :] = out.astype(bf16)
    sums_ref[:local] = sum(
        jnp.sum(ref[...].astype(f32), axis=1, keepdims=True) for ref in d_query_refs
    )
    sums_ref[local:] = jnp.sum(d_kv_ref[...].astype(f32), axis=1, keepdims=True)
    if len(keep_ref.shape) == 2:
        keep_ref[...] = out_ref[...]
    else:
        core = core_ref[0]
        chips, piece_rows, _ = keep_ref.shape
        for chip in range(chips):
            kept = pl.multiple_of((2 * chip + core) * piece_rows, 16)
            sent = pl.multiple_of((2 * chip + 1 - core) * piece_rows, 16)
            keep_ref[chip] = out_ref[pl.ds(kept, piece_rows)]
            send_ref[chip] = out_ref[pl.ds(sent, piece_rows)]


def attn_gradients(attn_in, d_kv, d_query, d_branch_rows, attended, core, chips):
    width = attn_in.shape[1]
    local = d_query[0].shape[0]
    rows = 4 * local // (2 * chips)
    part = jax.ShapeDtypeStruct((chips, rows, width), bf16)
    if rows % 16:
        parts = (jax.ShapeDtypeStruct((4 * local, width), bf16), jax.ShapeDtypeStruct((8, 128), bf16))
    else:
        parts = (part, part)
    keep, send, sums = kernel_call(
        functools.partial(attn_gradient_kernel, len(d_query)),
        (*parts, jax.ShapeDtypeStruct((3 * local, 1), f32)),
        in_specs=[SMEM_SPEC] + [VMEM_SPEC] * (2 + 2 * len(d_query) + len(attended)),
        out_specs=(VMEM_SPEC, VMEM_SPEC, VMEM_SPEC),
        scratch_shapes=[pltpu.VMEM((4 * local, width), bf16)],
    )(core.reshape(1), attn_in, d_kv, *d_query, *d_branch_rows, *attended)
    if rows % 16:
        both = keep.reshape(chips, 2, rows, width)
        keep = lax.dynamic_index_in_dim(both, core, 1, keepdims=False)
        send = lax.dynamic_index_in_dim(both, 1 - core, 1, keepdims=False)
    return (keep, send), sums


def attn_outputs_kernel(core_ref, own_ref, other_ref, *out_refs):
    core = core_ref[0]
    rows = own_ref.shape[1]
    for at, ref in enumerate(out_refs):
        ref[pl.ds(pl.multiple_of(core * rows, 16), rows)] = own_ref[at].astype(f32)
        ref[pl.ds(pl.multiple_of((1 - core) * rows, 16), rows)] = other_ref[at].astype(f32)


def attn_outputs(own, other, core):
    chips, rows, width = own.shape
    if chips != 4 or rows % 16:
        both = jnp.where(core == 0, jnp.stack([own, other], 1), jnp.stack([other, own], 1))
        q, k, v, o = jnp.split(both.astype(f32).reshape(-1, width), 4)
    else:
        part = jax.ShapeDtypeStruct((2 * rows, width), f32)
        q, k, v, o = kernel_call(
            attn_outputs_kernel,
            [part] * 4,
            in_specs=[SMEM_SPEC, VMEM_SPEC, VMEM_SPEC],
            out_specs=[VMEM_SPEC] * 4,
        )(core.reshape(1), own, other)
    return q.T, k.T, v.T, o


def split_pieces_kernel(chip_ref, keep_ref, flipped_ref, own_ref, *send_refs):
    for mask, ref in enumerate((own_ref, *send_refs)):
        chip = chip_ref[0] ^ mask
        ref[...] = (keep_ref[chip].astype(f32) + flipped_ref[chip].astype(f32)).astype(bf16)


def split_pieces(keep, flipped, chip):
    piece = jax.ShapeDtypeStruct(keep.shape[1:], bf16)
    return kernel_call(
        split_pieces_kernel,
        [piece] * keep.shape[0],
        in_specs=[SMEM_SPEC, VMEM_SPEC, VMEM_SPEC],
        out_specs=[VMEM_SPEC] * keep.shape[0],
    )(chip.reshape(1), keep, flipped)


def add_kernel(*refs):
    total = sum([ref[...].astype(f32) for ref in refs[1:-1]], refs[0][...].astype(f32))
    refs[-1][...] = total.astype(bf16)


def add_arrays(*arrays):
    return kernel_call(
        add_kernel,
        jax.ShapeDtypeStruct(arrays[0].shape, bf16),
        in_specs=[VMEM_SPEC] * len(arrays),
        out_specs=VMEM_SPEC,
    )(*arrays)


def cut_kernel(in_ref, *out_refs):
    for at, ref in enumerate(out_refs):
        ref[...] = in_ref[at]


def cut(array):
    part = jax.ShapeDtypeStruct(array.shape[1:], array.dtype)
    return kernel_call(
        cut_kernel, [part] * array.shape[0], in_specs=[VMEM_SPEC], out_specs=[VMEM_SPEC] * array.shape[0]
    )(array)


def collect_kernel(chip_ref, *refs):
    for mask, ref in enumerate(refs[:-1]):
        refs[-1][chip_ref[0] ^ mask] = ref[...]


def collect(pieces, chip):
    return kernel_call(
        collect_kernel,
        jax.ShapeDtypeStruct((len(pieces), *pieces[0].shape), pieces[0].dtype),
        in_specs=[SMEM_SPEC] + [VMEM_SPEC] * len(pieces),
        out_specs=VMEM_SPEC,
    )(chip.reshape(1), *pieces)


def mlp_outputs_kernel(in_ref, up_ref, down_ref):
    up_ref[...] = in_ref[0, 0].astype(f32)
    down_ref[...] = in_ref[0, 1].astype(f32)


def mlp_outputs(grad, up_shape):
    pieces, _, rows, width = grad.shape
    hidden_local = pieces * rows
    if rows % 16:
        up, down = grad[:, 0].astype(f32), grad[:, 1].astype(f32)
    else:
        spec = pl.BlockSpec((rows, width), lambda index: (index, 0))
        out = jax.ShapeDtypeStruct((hidden_local, width), f32)
        up, down = kernel_call(
            mlp_outputs_kernel,
            [out, out],
            grid=(pieces,),
            in_specs=[pl.BlockSpec((1, 2, rows, width), lambda index: (index, 0, 0, 0))],
            out_specs=[spec, spec],
        )(grad)
    return up.reshape(up_shape), down.reshape(hidden_local, width)


def shards(
    tokens,
    condition,
    q_weight,
    q_bias,
    k_weight,
    v_weight,
    v_bias,
    o_weight,
    o_bias,
    up_weight,
    up_bias,
    down_weight,
    down_bias,
    ada_weight,
    ada_bias,
    out_grad,
    slot_clip,
    clip_patches,
):
    n_narrow = lax.axis_size("narrow")
    n_wide = lax.axis_size("wide")
    own_rows, width = tokens.shape
    clip_count = condition.shape[0]
    local = q_weight.shape[1]
    hidden_local = up_weight.shape[1]
    slot_count = slot_clip.shape[0]
    members = PATCH_HI // own_rows
    assert members * slot_count == n_narrow
    narrow_index = lax.axis_index("narrow")
    wide_index = lax.axis_index("wide")
    slot = narrow_index // members
    clip = slot_clip[slot]
    patches = clip_patches[clip].reshape(1)
    others = list(range(1, members))
    other_shards = list(range(1, slot_count))

    def member_of(at, step):
        return at // members * members + (at + step) % members

    def fetch_rows(array, step):
        return lax.ppermute(
            array, "narrow", [(member_of(at, step), at) for at in range(n_narrow)]
        )

    def send_rows(array, step):
        return lax.ppermute(
            array, "narrow", [(at, member_of(at, step)) for at in range(n_narrow)]
        )

    def fetch_shard(array, step):
        return lax.ppermute(
            array,
            "narrow",
            [((at + step * members) % n_narrow, at) for at in range(n_narrow)],
        )

    def send_shard(array, step):
        return lax.ppermute(
            array,
            "narrow",
            [(at, (at + step * members) % n_narrow) for at in range(n_narrow)],
        )

    def after(value, *earlier):
        return lax.optimization_barrier((value, *earlier))[0]

    def piece(weight):
        rows = weight.shape[0] // n_wide
        return lax.dynamic_slice_in_dim(weight, wide_index * rows, rows, 0)

    def gathered(pieces):
        return [lax.all_gather(each, "wide", axis=0, tiled=True) for each in pieces]

    def fetched(pack):
        return [fetch_shard(pack, step) for step in other_shards]

    own_pack = jnp.concatenate([q_weight.T, k_weight.T, v_weight.T, o_weight], axis=0)
    own_piece = piece(own_pack)
    attn_pieces = fetched(own_piece)
    bias_pack = jnp.concatenate([q_bias, jnp.zeros_like(q_bias), v_bias, up_bias])
    bias_packs = [bias_pack] + fetched(bias_pack)
    sent_tokens = after(tokens, own_piece)
    token_rows = [tokens] + [fetch_rows(sent_tokens, step) for step in others]

    cond_float = condition.astype(f32)
    silu_cond = jax.nn.silu(cond_float).astype(bf16)
    mod_part = (
        jnp.einsum("cd,dke->cke", silu_cond[slot_clip], ada_weight, preferred_element_type=f32)
        + ada_bias
    )
    mod_blocks = []
    for step in range(n_narrow):
        target = (narrow_index + step) % n_narrow
        block = lax.dynamic_index_in_dim(mod_part, target // members, 0, keepdims=False)
        if step:
            block = lax.ppermute(
                block, "narrow", [(at, (at + step) % n_narrow) for at in range(n_narrow)]
            )
        mod_blocks.append(block)
    mod_slot = jnp.roll(jnp.stack(mod_blocks[::-1]), narrow_index + 1, axis=0)
    modulation = mod_slot.transpose(1, 0, 2).reshape(6, width)

    packs = [own_pack]
    packs += gathered(
        [after(each, mod_part, token_rows[-1], *bias_packs[1:]) for each in attn_pieces]
    )
    qkv_biases = [pack[: 3 * local] for pack in bias_packs]
    up_biases = jnp.stack([pack[3 * local :] for pack in bias_packs]).reshape(slot_count, 1, -1)

    attn_in = modulated_rows(token_rows, modulation)
    qkv = [qkv_rows(attn_in, packs[0], qkv_biases[0])]

    flat_shape = (hidden_local, width)
    mlp_pack = jnp.concatenate([piece(up_weight.reshape(flat_shape)), piece(down_weight)], axis=1)
    mlp_pack = after(mlp_pack, token_rows[-1], modulation)
    mlp_pieces = fetched(mlp_pack)
    own_grad = after(out_grad, *mlp_pieces)
    grad_rows = [own_grad] + [fetch_rows(own_grad, step) for step in others]

    half_rows = max(own_rows // 2, BLOCK)
    halves_of = {block: own_rows // half_rows for block in others}
    halves_of[0] = 1
    attended = [{} for _ in range(slot_count)]
    lse = [{} for _ in range(slot_count)]
    attended_turned = [{} for _ in range(slot_count)]

    def attend(index, block, half, *earlier):
        rows = own_rows // halves_of[block]
        results = attention_forward(
            after(qkv[index], *earlier), patches, block * own_rows + half * rows, rows
        )
        for kept, result in zip((attended, attended_turned, lse), results):
            kept[index][block, half] = result
        return results[0]

    parts_of = [(block, half) for block in others for half in range(halves_of[block])]
    for part in parts_of:
        last_rows = attend(0, *part)
    mlp_packs = gathered([after(each, last_rows) for each in mlp_pieces])
    for index in other_shards:
        rows = after(attn_in, last_rows)
        qkv.append(qkv_rows(rows, packs[index], qkv_biases[index]))

    def branch_sum(rows, pack_refs):
        return sum(dot(each, ref[3 * local :]) for each, ref in zip(rows, pack_refs))

    zero_row = jnp.zeros((1, width), f32)
    def branch_part(part, kind):
        rows = [parts[part] for parts in attended]
        return row_call(
            lambda rows, vectors: ([branch_sum(rows, vectors[1:])], []), rows, [zero_row, *packs], [kind]
        )[0]

    arrived = {}
    earlier = []
    for part in parts_of:
        for index in other_shards:
            attend(index, *part, *earlier)
        earlier = [branch_part(part, bf16)]
        arrived[part] = send_rows(earlier[0], part[0])
    last_rows = attend(0, 0, 0, *earlier)
    for index in other_shards:
        last_rows = attend(index, 0, 0, last_rows, *grad_rows[1:])
    own_branch = branch_part((0, 0), f32)

    def joined(parts, axis=0):
        parts = list(parts)
        return parts[0] if len(parts) == 1 else jnp.concatenate(parts, axis=axis)

    def blocks_of(parts, axis):
        return [
            joined((parts[block, half] for half in range(halves_of[block])), axis)
            for block in range(members)
        ]

    lse = [blocks_of(parts, 1) for parts in lse]
    attended_turned = [
        [parts[block, half] for block in range(members) for half in range(halves_of[block])]
        for parts in attended_turned
    ]
    arrived = [
        joined(after(arrived[block, half], own_branch) for half in range(halves_of[block]))
        for block in others
    ]

    def middle_body(rows, vectors):
        token, *rest = [each.astype(f32) for each in rows]
        mod_ref, bias_ref = vectors
        branch = sum(rest[1:], rest[0]) + bias_ref[...].astype(f32)
        normed = normalize(token + mod_ref[2:3] * branch)[0]
        return [branch, normed * (1.0 + mod_ref[4:5]) + mod_ref[3:4]], []

    branch_one, mlp_own = row_call(
        middle_body,
        [tokens, own_branch, *arrived],
        [modulation, o_bias.reshape(1, width)],
        [f32, bf16],
    )

    mlp_rows = [mlp_own] + [fetch_rows(mlp_own, step) for step in others]
    ups, downs = [(up_weight, 0)], [(down_weight, 0)]
    for pack in mlp_packs:
        if hidden_local == width and hidden_local % HIDDEN_BLOCK == 0:
            ups.append((pack, 0))
            downs.append((pack, 1))
        else:
            ups.append((pack[:, :width].reshape(up_weight.shape), 0))
            downs.append((pack[:, width:], 0))
    hidden, d_pre, d_branch_two, d_mlp, branch_two, bias_sums_up = [], [], [], [], [], []
    for block in range(members):
        rows = after(mlp_rows[block], *d_mlp)
        results = feed_forward(
            rows, grad_rows[block], modulation, up_biases, ups, downs, bf16 if block else f32
        )
        for kept, result in zip((hidden, d_pre, d_branch_two, d_mlp, branch_two, bias_sums_up), results):
            kept.append(result)
    arrived = [send_rows(d_mlp[block], block) for block in others]
    grad_mlp_part = mlp_gradients(mlp_rows, d_branch_two, hidden, d_pre, n_wide)
    up_bias_sums = sum(bias_sums_up)[:slot_count]

    def d_middle_body(rows, vectors):
        token, branch, grad, *parts = [each.astype(f32) for each in rows]
        (mod_ref,) = vectors
        d_mlp_in = sum(parts[1:], parts[0])
        normed, inverse = normalize(token + mod_ref[2:3] * branch)
        d_middle = grad + norm_back(d_mlp_in * (1.0 + mod_ref[4:5]), normed, inverse)
        d_branch_one = (mod_ref[2:3] * d_middle).astype(bf16)
        terms = [d_middle * branch, d_mlp_in, d_mlp_in * normed, d_branch_one.astype(f32)]
        return [d_branch_one, d_middle], terms

    arrived = [after(part, grad_mlp_part) for part in arrived]
    d_branch_one, d_middle, middle_sums = row_call(
        d_middle_body, [tokens, branch_one, out_grad, d_mlp[0], *arrived], [modulation], [bf16, f32], 4
    )
    mlp_scattered = lax.psum_scatter(after(grad_mlp_part, *arrived), "wide", scatter_dimension=0, tiled=True)
    d_branch_rows = [d_branch_one] + [fetch_rows(d_branch_one, step) for step in others]

    assert n_wide & (n_wide - 1) == 0
    bits = n_wide.bit_length() - 1
    chips = n_wide // 2
    core, chip = wide_index % 2, wide_index // 2

    def wide_xor(array, mask):
        return lax.ppermute(array, "wide", [(at, at ^ mask) for at in range(n_wide)])

    def start_cores(part):
        keep, send = part
        return keep, wide_xor(send, 1)

    def end_cores(started):
        return split_pieces(*started, chip)

    def start_chips(pieces):
        return [pieces[0]] + [wide_xor(each, 2 * mask) for mask, each in enumerate(pieces[1:], 1)]

    shard_order = other_shards + [0]
    d_query = [[None] * members for _ in range(slot_count)]
    d_query_turned = [[None] * members for _ in range(slot_count)]
    d_kv, d_kv_turned = [None] * slot_count, [None] * slot_count
    grad_attn_part, attn_bias_sums = [None] * slot_count, [None] * slot_count

    def attn_gradients_of(index, *earlier):
        grad_attn_part[index], attn_bias_sums[index] = attn_gradients(
            attn_in,
            after(d_kv_turned[index], *earlier),
            d_query_turned[index],
            d_branch_rows,
            attended_turned[index],
            core,
            chips,
        )

    for block in range(members):
        last = block == members - 1
        for index in shard_order:
            d_query[index][block], d_query_turned[index][block], d_kv[index], *turned = (
                attention_backward(
                    qkv[index],
                    d_branch_rows[block],
                    packs[index],
                    lse[index][block],
                    patches,
                    d_kv[index],
                    block * own_rows,
                    last,
                )
            )
            if last:
                d_kv_turned[index] = turned[0]
                if index:
                    attn_gradients_of(index)
                    d_branch_rows[block] = after(d_branch_rows[block], grad_attn_part[index][0])
        if not last:
            d_branch_rows[block + 1] = after(d_branch_rows[block + 1], d_kv[0])

    def d_attn_sum(rows, pack_refs):
        total = 0.0
        for index, ref in enumerate(pack_refs):
            total = total + dot(rows[2 * index], ref[:local])
            total = total + dot(rows[2 * index + 1], ref[local : 3 * local])
        return total

    def d_rows_of(block):
        rows = []
        for index in range(slot_count):
            rows += [d_query[index][block], (d_kv[index], block * own_rows)]
        return rows

    cores_ended = [end_cores(start_cores(part)) for part in grad_attn_part[1:]]
    chips_started_of = {index: start_chips(cores_ended[index - 1]) for index in other_shards}
    mlp_scattered = after(mlp_scattered, d_kv[0])
    mlp_sent = cut(mlp_scattered.reshape(slot_count, 2, -1, width))
    mlp_arrived = [send_shard(mlp_sent[step], step) for step in other_shards]
    attn_gradients_of(0, *mlp_sent[1:], *(pieces[0] for pieces in cores_ended))
    d_kv[0] = after(d_kv[0], grad_attn_part[0][0])
    def d_attn_part(block, kind):
        return row_call(
            lambda rows, vectors: ([d_attn_sum(rows, vectors[1:])], []),
            d_rows_of(block),
            [zero_row, *packs],
            [kind],
        )[0]

    d_attn_parts = [d_attn_part(block, bf16) for block in others]
    arrived = [send_rows(part, block) for part, block in zip(d_attn_parts, others)]
    own_cores = start_cores(grad_attn_part[0])

    late_branch = [after(branch_two[block], *d_branch_rows[1:]) for block in others]
    arrived_two = [send_rows(part, block) for part, block in zip(late_branch, others)]
    arrived_two = [after(part, *d_attn_parts) for part in arrived_two]

    def out_body(rows, vectors):
        token, branch, grad, *parts = [each.astype(f32) for each in rows]
        mod_ref, bias_ref = vectors
        total = sum(parts[1:], parts[0]) + bias_ref[...].astype(f32)
        block_out = token + mod_ref[2:3] * branch + mod_ref[5:6] * total
        return [block_out], [grad * total, (mod_ref[5:6] * grad).astype(bf16).astype(f32)]

    block_out, out_sums = row_call(
        out_body,
        [tokens, branch_one, out_grad, branch_two[0], *arrived_two],
        [modulation, down_bias.reshape(1, width)],
        [bf16],
        2,
    )
    d_query[0][0] = after(d_query[0][0], block_out)
    own_d_attn = d_attn_part(0, f32)
    def end_body(rows, vectors):
        token, d_middle_rows, *parts = rows
        (mod_ref,) = vectors
        d_attn_in = sum([each.astype(f32) for each in parts[1:]], parts[0])
        normed, inverse = normalize(token.astype(f32))
        grad = d_middle_rows + norm_back(d_attn_in * (1.0 + mod_ref[1:2]), normed, inverse)
        return [grad], [d_attn_in, d_attn_in * normed]

    piece_sums = []
    for index in other_shards:
        own, *pieces = chips_started_of[index]
        piece_sums.append(add_arrays(own, *(after(each, own_d_attn) for each in pieces)))
    own_pieces = end_cores((own_cores[0], after(own_cores[1], *d_attn_parts)))
    chips_started = start_chips(own_pieces)
    arrived = [after(part, own_d_attn, own_pieces[0], *piece_sums) for part in arrived]
    grad_tokens, end_sums = row_call(
        end_body, [tokens, d_middle, own_d_attn, *arrived], [modulation], [f32], 2
    )

    sent = [send_shard(each, index) for index, each in zip(other_shards, piece_sums)]
    mlp_total = add_arrays(mlp_sent[0], *(after(each, own_d_attn) for each in mlp_arrived))

    own_sums = jnp.concatenate(
        [end_sums[0:2], middle_sums[0:3], out_sums[0:1], middle_sums[3:4], out_sums[1:2]]
    )
    bit = 1
    while bit < members:
        own_sums = own_sums + lax.ppermute(
            own_sums, "narrow", [(at, at ^ bit) for at in range(n_narrow)]
        )
        bit *= 2
    shard_parts = [
        jnp.concatenate([attn_bias_sums[step].reshape(-1), up_bias_sums[step]])
        for step in range(slot_count)
    ]
    slot_sums = [own_sums] + [fetch_shard(own_sums, step) for step in other_shards]
    shard_parts[1:] = [send_shard(shard_parts[step], step) for step in other_shards]
    total = add_arrays(*chips_started, *sent)

    grad_mlp = lax.all_gather(mlp_total, "wide", axis=0, tiled=False)
    grad_up_weight, grad_down_weight = mlp_outputs(grad_mlp, up_weight.shape)

    pieces = collect([total] + [wide_xor(total, 2 * mask) for mask in range(1, chips)], chip)
    flipped_pieces = wide_xor(pieces, 1)

    clip_ids = jnp.arange(clip_count, dtype=jnp.int32)
    d_mod_clips = jnp.zeros((clip_count, 6, local), f32)
    bias_sums = jnp.zeros((2, width), f32)
    shard_sum = jnp.zeros((3 * local + hidden_local,), f32)
    for step in range(slot_count):
        source_clip = slot_clip[(slot + step) % slot_count]
        one_hot = (clip_ids == source_clip).astype(f32)
        columns = lax.dynamic_slice_in_dim(slot_sums[step][:6], narrow_index * local, local, 1)
        d_mod_clips = d_mod_clips + one_hot[:, None, None] * columns
        bias_sums = bias_sums + slot_sums[step][6:]
        shard_sum = shard_sum + shard_parts[step]
    small = jnp.concatenate([d_mod_clips.reshape(-1), bias_sums.reshape(-1), shard_sum])
    for bit in range(bits):
        small = small + wide_xor(small, 1 << bit)
    grad_q_weight, grad_k_weight, grad_v_weight, grad_o_weight = attn_outputs(
        pieces, flipped_pieces, core
    )
    mod_size = clip_count * 6 * local
    d_modulation = small[:mod_size].reshape(clip_count, 6, local)
    grad_o_bias = small[mod_size : mod_size + width]
    grad_down_bias = small[mod_size + width : mod_size + 2 * width]
    shard_sum = small[mod_size + 2 * width :]
    grad_q_bias = shard_sum[:local]
    grad_v_bias = shard_sum[2 * local : 3 * local]
    grad_up_bias = shard_sum[3 * local :]

    silu_float = silu_cond.astype(f32)
    grad_ada_weight = jnp.einsum("cd,cke->dke", silu_float, d_modulation, precision=highest)
    grad_ada_bias = jnp.sum(d_modulation, axis=0)
    d_silu = jnp.einsum(
        "cke,dke->cd", d_modulation, ada_weight.astype(f32), precision=highest
    )
    bit = 1
    while bit < n_narrow:
        d_silu = d_silu + lax.ppermute(d_silu, "narrow", [(at, at ^ bit) for at in range(n_narrow)])
        bit *= 2
    grad_condition = jax.vjp(jax.nn.silu, cond_float)[1](d_silu)[0]
    return (
        block_out,
        grad_tokens,
        grad_condition,
        grad_q_weight,
        grad_q_bias,
        grad_k_weight,
        grad_v_weight,
        grad_v_bias,
        grad_o_weight,
        grad_o_bias,
        grad_up_weight,
        grad_up_bias,
        grad_down_weight,
        grad_down_bias,
        grad_ada_weight,
        grad_ada_bias,
    )


def solution(mesh):
    in_specs = (
        P(("wide", "narrow"), None),
        P(),
        P(None, "narrow"),
        P("narrow"),
        P(None, "narrow"),
        P(None, "narrow"),
        P("narrow"),
        P("narrow", None),
        P(),
        P(None, "narrow"),
        P("narrow"),
        P("narrow", None),
        P(),
        P(None, None, "narrow"),
        P(None, "narrow"),
        P(("wide", "narrow"), None),
        P("wide"),
        P(),
    )
    out_specs = (
        P(("wide", "narrow"), None),
        P(("wide", "narrow"), None),
        P(),
        P(None, "narrow"),
        P("narrow"),
        P(None, "narrow"),
        P(None, "narrow"),
        P("narrow"),
        P("narrow", None),
        P(),
        P(None, "narrow"),
        P("narrow"),
        P("narrow", None),
        P(),
        P(None, None, "narrow"),
        P(None, "narrow"),
    )
    return jax.shard_map(shards, mesh=mesh, in_specs=in_specs, out_specs=out_specs, check_vma=False)
```

```python
import functools

import jax
import jax.numpy as jnp
from jax import lax
from jax.experimental import pallas as pl
from jax.experimental.pallas import tpu as pltpu
from jax.sharding import PartitionSpec as P

HDIM = 72
PATCH_HI = 1024
BLOCK = 256
ROW_BLOCK = 256
HIDDEN_BLOCK = 384
VMEM_LIMIT = 48 * 1024 * 1024

epsilon = 1e-06
highest = lax.Precision.HIGHEST
EXP2_SCALE = HDIM ** (-0.5) * 1.4426950408889634
f32 = jnp.float32
bf16 = jnp.bfloat16


def normalize(row_block):
    centred = row_block - jnp.mean(row_block, axis=-1, keepdims=True)
    variance = jnp.mean(centred * centred, axis=-1, keepdims=True)
    inverse = lax.rsqrt(variance + epsilon)
    return (centred * inverse, inverse)


def norm_back(d_normed, normed, inverse):
    first_mean = jnp.mean(d_normed, axis=-1, keepdims=True)
    second_mean = jnp.mean(d_normed * normed, axis=-1, keepdims=True)
    return inverse * (d_normed - first_mean - normed * second_mean)


def gelu_and_slope(values):
    root = (2.0 / jnp.pi) ** 0.5
    square = values * values
    tanh = jnp.tanh(root * (values + 0.044715 * (square * values)))
    half = 0.5 * (1.0 + tanh)
    slope = half + 0.5 * values * (1.0 - tanh * tanh) * (root + (3 * 0.044715 * root) * square)
    return values * half, slope


def dot(left, right):
    return jnp.dot(left, right, preferred_element_type=f32)


def dot_t(left, right):
    return lax.dot_general(left, right, (((1,), (1,)), ((), ())), preferred_element_type=f32)


def contract_rows(left, right):
    return lax.dot_general(left, right, (((0,), (0,)), ((), ())), preferred_element_type=f32)


def left_t_right_t(left, right):
    return lax.dot_general(left, right, (((0,), (1,)), ((), ())), preferred_element_type=f32)


def kernel_call(kernel, outs, **options):
    return pl.pallas_call(
        kernel,
        out_shape=outs,
        compiler_params=pltpu.CompilerParams(vmem_limit_bytes=VMEM_LIMIT),
        cost_estimate=pl.CostEstimate(flops=0, bytes_accessed=1024, transcendentals=0),
        **options,
    )


def whole(array):
    return pl.BlockSpec(array.shape, lambda *_: (0,) * len(array.shape))


def row_call(body, rows_in, vectors, out_types, term_count=0):
    rows, width = rows_in[0].shape[0], vectors[0].shape[1]
    step_rows = min(ROW_BLOCK, rows)
    rows_in = [each if isinstance(each, tuple) else (each, 0) for each in rows_in]

    def kernel(*refs):
        row_refs = refs[: len(rows_in)]
        vector_refs = refs[len(rows_in) : len(rows_in) + len(vectors)]
        out_refs = refs[len(rows_in) + len(vectors) :]
        outs, terms = body([ref[...] for ref in row_refs], vector_refs)
        for ref, out in zip(out_refs, outs):
            ref[...] = out.astype(ref.dtype)
        if term_count:
            sums_ref = refs[-1]

            @pl.when(pl.program_id(0) == 0)
            def _():
                sums_ref[...] = jnp.zeros_like(sums_ref)

            for index, term in enumerate(terms):
                sums_ref[index : index + 1, :] += jnp.sum(term, axis=0, keepdims=True)

    outs = [jax.ShapeDtypeStruct((rows, width), kind) for kind in out_types]
    out_specs = [pl.BlockSpec((step_rows, width), lambda index: (index, 0))] * len(outs)
    if term_count:
        outs.append(jax.ShapeDtypeStruct((8, width), f32))
        out_specs.append(pl.BlockSpec((8, width), lambda index: (0, 0)))
    return kernel_call(
        kernel,
        outs,
        grid=(rows // step_rows,),
        in_specs=[
            pl.BlockSpec((step_rows, each.shape[1]), lambda index, first=first: (first // step_rows + index, 0))
            for each, first in rows_in
        ]
        + [whole(each) for each in vectors],
        out_specs=out_specs,
    )(*(each for each, _ in rows_in), *vectors)


def modulated_rows_kernel(row_count, *refs):
    mod_ref, out_ref = refs[-2:]
    for index, ref in enumerate(refs[:row_count]):
        normed = normalize(ref[...].astype(f32))[0]
        out_ref[index] = (normed * (1.0 + mod_ref[1:2, :]) + mod_ref[0:1, :]).astype(bf16)


def modulated_rows(row_blocks, modulation):
    rows, width = row_blocks[0].shape
    count = len(row_blocks)
    out = kernel_call(
        functools.partial(modulated_rows_kernel, count),
        jax.ShapeDtypeStruct((count, rows, width), bf16),
        grid=(rows // ROW_BLOCK,),
        in_specs=[pl.BlockSpec((ROW_BLOCK, width), lambda index: (index, 0))] * count
        + [whole(modulation)],
        out_specs=pl.BlockSpec((count, ROW_BLOCK, width), lambda index: (0, index, 0)),
    )(*row_blocks, modulation)
    return out.reshape(count * rows, width)


def qkv_kernel(rows_ref, pack_ref, bias_ref, out_ref):
    columns = out_ref.shape[1]
    rows = dot_t(rows_ref[...], pack_ref[:columns]) + bias_ref[...].astype(f32)
    out_ref[...] = rows.astype(bf16)


def qkv_rows(rows, pack, bias):
    columns = pack.shape[0] // 4 * 3
    bias = bias.reshape(1, columns)
    return kernel_call(
        qkv_kernel,
        jax.ShapeDtypeStruct((rows.shape[0], columns), bf16),
        grid=(2,),
        in_specs=[
            pl.BlockSpec((rows.shape[0] // 2, rows.shape[1]), lambda index: (index, 0)),
            whole(pack),
            whole(bias),
        ],
        out_specs=pl.BlockSpec((rows.shape[0] // 2, columns), lambda index: (index, 0)),
    )(rows, pack, bias)


def frame_loop(patches_ref, rows, heads, stages):
    is_full = patches_ref[0] == PATCH_HI
    first, second, third = stages

    def run(full):
        units = [(block * BLOCK, head) for block in range(rows // BLOCK) for head in range(heads)]
        begun = first(*units[0], full)
        done = None
        for at, unit in enumerate(units):
            coming = first(*units[at + 1], full) if at + 1 < len(units) else None
            if done is not None:
                third(*units[at - 1], full, done)
            done = second(*unit, full, begun)
            begun = coming
        third(*units[-1], full, done)

    @pl.when(is_full)
    def _():
        run(True)

    @pl.when(jnp.logical_not(is_full))
    def _():
        run(False)


def attention_forward_kernel(
    first_row, patches_ref, qkv_ref, attended_ref, turned_ref, lse_ref, out_scratch
):
    heads = qkv_ref.shape[1] // (3 * HDIM)

    def columns(start, full, part, head):
        at = (part * heads + head) * HDIM
        rows = slice(0, PATCH_HI) if full else slice(first_row + start, first_row + start + BLOCK)
        return qkv_ref[rows, at : at + HDIM]

    def scores(start, head, full):
        return dot_t(columns(start, full, 1, head), columns(start, False, 0, head))

    def softmax(start, head, full, logits):
        out_rows = slice(start, start + BLOCK)
        top = jnp.max(logits, axis=0, keepdims=True) * EXP2_SCALE
        exp_scores = jnp.exp2(logits * EXP2_SCALE - top)
        total = jnp.sum(exp_scores, axis=0, keepdims=True)
        lse_ref[head : head + 1, out_rows] = top + jnp.log2(total)
        return (exp_scores * (1.0 / total)).astype(bf16)

    def values(start, head, full, weights):
        out_scratch[head * HDIM : (head + 1) * HDIM, start : start + BLOCK] = contract_rows(
            columns(start, full, 2, head), weights
        )

    frame_loop(patches_ref, lse_ref.shape[1], heads, (scores, softmax, values))
    attended_ref[...] = out_scratch[...].T.astype(bf16)
    turned_ref[...] = out_scratch[...].astype(bf16)


VMEM_SPEC = pl.BlockSpec(memory_space=pltpu.VMEM)
SMEM_SPEC = pl.BlockSpec(memory_space=pltpu.SMEM)


def attention_forward(qkv, patches, first_row, rows):
    width = qkv.shape[1] // 3
    return kernel_call(
        functools.partial(attention_forward_kernel, first_row),
        (
            jax.ShapeDtypeStruct((rows, width), bf16),
            jax.ShapeDtypeStruct((width, rows), bf16),
            jax.ShapeDtypeStruct((width // HDIM, rows), f32),
        ),
        in_specs=[SMEM_SPEC, VMEM_SPEC],
        out_specs=(VMEM_SPEC, VMEM_SPEC, VMEM_SPEC),
        scratch_shapes=[pltpu.VMEM((width, rows), f32)],
    )(patches, qkv)


def attention_backward_kernel(first_row, first, last, *refs):
    patches_ref, qkv_ref, d_rows_ref, pack_ref, lse_ref = refs[:5]
    sums_ref = refs[5] if not first else None
    d_query_ref, d_query_turned_ref, d_kv_ref, *rest = refs[5 if first else 6 :]
    d_kv_turned_ref = rest[0] if last else None
    query_scratch, kv_scratch, d_scratch = rest[-3:]
    local = d_query_ref.shape[1]
    heads = local // HDIM
    scale = HDIM ** (-0.5)
    kv_scratch[...] = jnp.zeros_like(kv_scratch) if first else sums_ref[...]
    d_scratch[...] = dot_t(d_rows_ref[...], pack_ref[3 * local :]).astype(bf16)

    def columns(start, full, part, head):
        at = (part * heads + head) * HDIM
        rows = slice(0, PATCH_HI) if full else slice(first_row + start, first_row + start + BLOCK)
        return qkv_ref[rows, at : at + HDIM]

    def d_out(start, head):
        return d_scratch[start : start + BLOCK, head * HDIM : (head + 1) * HDIM]

    def products(start, head, full):
        logits = dot_t(columns(start, full, 1, head), columns(start, False, 0, head))
        return logits, dot_t(columns(start, full, 2, head), d_out(start, head))

    def d_softmax(start, head, full, pair):
        logits, d_weights = pair
        probs = jnp.exp2(logits * EXP2_SCALE - lse_ref[head : head + 1, start : start + BLOCK])
        delta = jnp.sum(probs * d_weights, axis=0, keepdims=True)
        return probs.astype(bf16), (probs * (d_weights - delta)).astype(bf16)

    def gradients(start, head, full, pair):
        probs, d_scores = pair
        at = slice(head * HDIM, (head + 1) * HDIM)
        v_at = slice(local + head * HDIM, local + (head + 1) * HDIM)
        k_rows = slice(0, PATCH_HI) if full else slice(first_row + start, first_row + start + BLOCK)
        query_scratch[at, start : start + BLOCK] = (
            contract_rows(columns(start, full, 1, head), d_scores) * scale
        )
        kv_scratch[at, k_rows] += left_t_right_t(columns(start, False, 0, head), d_scores) * scale
        kv_scratch[v_at, k_rows] += left_t_right_t(d_out(start, head), probs)

    frame_loop(patches_ref, lse_ref.shape[1], heads, (products, d_softmax, gradients))
    d_query_ref[...] = query_scratch[...].T.astype(bf16)
    d_query_turned_ref[...] = query_scratch[...].astype(bf16)
    if last:
        d_kv_ref[...] = kv_scratch[...].T.astype(bf16)
        d_kv_turned_ref[...] = kv_scratch[...].astype(bf16)
    else:
        d_kv_ref[...] = kv_scratch[...]


def attention_backward(qkv, d_rows, pack, lse, patches, sums, first_row, last):
    local = pack.shape[0] // 4
    rows = d_rows.shape[0]
    first = sums is None
    turned = (2 * local, PATCH_HI)
    extra = [] if first else [sums]
    outs = [jax.ShapeDtypeStruct((rows, local), bf16), jax.ShapeDtypeStruct((local, rows), bf16)]
    if last:
        outs += [jax.ShapeDtypeStruct(turned[::-1], bf16), jax.ShapeDtypeStruct(turned, bf16)]
    else:
        outs.append(jax.ShapeDtypeStruct(turned, f32))
    return kernel_call(
        functools.partial(attention_backward_kernel, first_row, first, last),
        outs,
        in_specs=[SMEM_SPEC] + [VMEM_SPEC] * (4 + len(extra)),
        out_specs=[VMEM_SPEC] * len(outs),
        scratch_shapes=[
            pltpu.VMEM((local, rows), f32),
            pltpu.VMEM(turned, f32),
            pltpu.VMEM((rows, local), bf16),
        ],
    )(patches, qkv, d_rows, pack, lse, *extra)


def feed_forward_kernel(last_types, shard_count, *refs):
    x_ref, grad_ref, mod_ref, bias_ref = refs[:4]
    up_refs = refs[4 : 4 + shard_count]
    down_refs = refs[4 + shard_count : 4 + 2 * shard_count]
    hidden_ref, d_pre_ref, d_branch_ref, d_mlp_ref, branch_ref, sums_ref = refs[-8:-2]
    d_mlp_scratch, branch_scratch = refs[-2:]

    @pl.when(pl.program_id(0) == 0)
    def _():
        d_mlp_scratch[...] = jnp.zeros_like(d_mlp_scratch)
        branch_scratch[...] = jnp.zeros_like(branch_scratch)
        d_branch_ref[...] = (mod_ref[5:6, :] * grad_ref[...].astype(f32)).astype(bf16)

    sums_ref[...] = jnp.zeros_like(sums_ref)

    def products(start, shard):
        block = slice(start, start + BLOCK)
        pre_act = dot(x_ref[block], up_refs[shard][...]) + bias_ref[shard].astype(f32)
        return pre_act, dot_t(d_branch_ref[block], down_refs[shard][...])

    def activation(start, shard, pair):
        block = slice(start, start + BLOCK)
        pre_act, d_hidden = pair
        hidden, slope = gelu_and_slope(pre_act)
        hidden, d_pre = hidden.astype(bf16), (d_hidden * slope).astype(bf16)
        hidden_ref[shard, block] = hidden
        d_pre_ref[shard, block] = d_pre
        sums_ref[shard : shard + 1] += jnp.sum(d_pre.astype(f32), axis=0, keepdims=True)
        return hidden, d_pre

    def add_sums(start, shard, pair):
        block = slice(start, start + BLOCK)
        hidden, d_pre = pair
        d_mlp_scratch[block] += dot_t(d_pre, up_refs[shard][...])
        branch_scratch[block] += dot(hidden, down_refs[shard][...])

    units = [
        (start, shard) for start in range(0, x_ref.shape[0], BLOCK) for shard in range(shard_count)
    ]
    begun, done = products(*units[0]), None
    for at, unit in enumerate(units):
        coming = products(*units[at + 1]) if at + 1 < len(units) else None
        if done is not None:
            add_sums(*units[at - 1], done)
        done = activation(*unit, begun)
        begun = coming
    add_sums(*units[-1], done)

    @pl.when(pl.program_id(0) == pl.num_programs(0) - 1)
    def _():
        d_mlp_ref[...] = d_mlp_scratch[...].astype(d_mlp_ref.dtype)
        branch_ref[...] = branch_scratch[...].astype(branch_ref.dtype)


def feed_forward(rows, grad, modulation, biases, ups, downs, sum_type):
    row_count, width = rows.shape
    shard_count = len(ups)
    hidden_local = biases.shape[-1]
    step = HIDDEN_BLOCK if hidden_local % HIDDEN_BLOCK == 0 else hidden_local
    in_specs = [whole(rows), whole(grad), whole(modulation)]
    in_specs.append(pl.BlockSpec((shard_count, 1, step), lambda index: (0, 0, index)))
    for _, first in ups:
        in_specs.append(pl.BlockSpec((width, step), lambda index, first=first: (0, first + index)))
    for _, first in downs:
        in_specs.append(pl.BlockSpec((step, width), lambda index, first=first: (index, first)))
    by_shard = pl.BlockSpec((shard_count, row_count, step), lambda index: (0, 0, index))
    flat = jax.ShapeDtypeStruct((row_count, width), sum_type)
    return kernel_call(
        functools.partial(feed_forward_kernel, sum_type, shard_count),
        [
            jax.ShapeDtypeStruct((shard_count, row_count, hidden_local), bf16),
            jax.ShapeDtypeStruct((shard_count, row_count, hidden_local), bf16),
            jax.ShapeDtypeStruct((row_count, width), bf16),
            flat,
            flat,
            jax.ShapeDtypeStruct((8, hidden_local), f32),
        ],
        grid=(hidden_local // step,),
        in_specs=in_specs,
        out_specs=[by_shard, by_shard]
        + [pl.BlockSpec((row_count, width), lambda index: (0, 0))] * 3
        + [pl.BlockSpec((8, step), lambda index: (0, index))],
        scratch_shapes=[pltpu.VMEM((row_count, width), f32)] * 2,
    )(rows, grad, modulation, biases, *(each for each, _ in ups), *(each for each, _ in downs))


def mlp_gradient_kernel(member_count, *refs):
    out_ref = refs[-1]
    is_up = pl.program_id(0) % 2 == 0
    pieces, _, rows, width = out_ref.shape

    def store(lefts, rights):
        total = sum(contract_rows(left, right) for left, right in zip(lefts, rights))
        out_ref[:, 0] = total.astype(bf16).reshape(pieces, rows, width)

    groups = [refs[at * member_count : (at + 1) * member_count] for at in range(4)]
    x_refs, d_branch_refs, hidden_refs, d_pre_refs = groups

    @pl.when(is_up)
    def _():
        store([ref[...] for ref in x_refs], [ref[0] for ref in d_pre_refs])

    @pl.when(jnp.logical_not(is_up))
    def _():
        store([ref[0] for ref in hidden_refs], [ref[...] for ref in d_branch_refs])


def mlp_gradients(x_rows, d_branch_rows, hidden, d_pre, pieces):
    shard_count, row_count, hidden_local = hidden[0].shape
    width = x_rows[0].shape[1]
    rows = hidden_local // pieces
    if hidden_local != width or rows % 16:
        parts = []
        for shard in range(shard_count):
            up = sum(contract_rows(left, right[shard]) for left, right in zip(x_rows, d_pre))
            down = sum(contract_rows(left[shard], right) for left, right in zip(hidden, d_branch_rows))
            parts += [up.reshape(pieces, rows, width), down.reshape(pieces, rows, width)]
        return jnp.stack(parts, axis=1).astype(bf16)
    by_shard = pl.BlockSpec((1, row_count, hidden_local), lambda index: (index // 2, 0, 0))
    return kernel_call(
        functools.partial(mlp_gradient_kernel, len(x_rows)),
        jax.ShapeDtypeStruct((pieces, 2 * shard_count, rows, width), bf16),
        grid=(2 * shard_count,),
        in_specs=[whole(each) for each in (*x_rows, *d_branch_rows)]
        + [by_shard] * (2 * len(x_rows)),
        out_specs=pl.BlockSpec((pieces, 1, rows, width), lambda index: (0, index, 0, 0)),
    )(*x_rows, *d_branch_rows, *hidden, *d_pre)


def attn_gradient_kernel(member_count, *refs):
    core_ref, in_ref, d_kv_ref = refs[:3]
    d_query_refs, d_branch_refs = refs[3 : 3 + member_count], refs[3 + member_count : 3 + 2 * member_count]
    attended_refs = refs[3 + 2 * member_count : -4]
    keep_ref, send_ref, sums_ref, out_ref = refs[-4:]
    local, rows = d_query_refs[0].shape
    query = sum(
        dot(ref[...], in_ref[at * rows : (at + 1) * rows]) for at, ref in enumerate(d_query_refs)
    )
    out_ref[:local] = query.astype(bf16)
    out_ref[local : 3 * local] = dot(d_kv_ref[...], in_ref[...]).astype(bf16)
    start, out = 0, 0.0
    for ref in attended_refs:
        first = start % rows
        out = out + dot(ref[...], d_branch_refs[start // rows][first : first + ref.shape[1]])
        start += ref.shape[1]
    out_ref[3 * local :] = out.astype(bf16)
    sums_ref[:local] = sum(
        jnp.sum(ref[...].astype(f32), axis=1, keepdims=True) for ref in d_query_refs
    )
    sums_ref[local:] = jnp.sum(d_kv_ref[...].astype(f32), axis=1, keepdims=True)
    if len(keep_ref.shape) == 2:
        keep_ref[...] = out_ref[...]
    else:
        core = core_ref[0]
        chips, piece_rows, _ = keep_ref.shape
        for chip in range(chips):
            kept = pl.multiple_of((2 * chip + core) * piece_rows, 16)
            sent = pl.multiple_of((2 * chip + 1 - core) * piece_rows, 16)
            keep_ref[chip] = out_ref[pl.ds(kept, piece_rows)]
            send_ref[chip] = out_ref[pl.ds(sent, piece_rows)]


def attn_gradients(attn_in, d_kv, d_query, d_branch_rows, attended, core, chips):
    width = attn_in.shape[1]
    local = d_query[0].shape[0]
    rows = 4 * local // (2 * chips)
    part = jax.ShapeDtypeStruct((chips, rows, width), bf16)
    if rows % 16:
        parts = (jax.ShapeDtypeStruct((4 * local, width), bf16), jax.ShapeDtypeStruct((8, 128), bf16))
    else:
        parts = (part, part)
    keep, send, sums = kernel_call(
        functools.partial(attn_gradient_kernel, len(d_query)),
        (*parts, jax.ShapeDtypeStruct((3 * local, 1), f32)),
        in_specs=[SMEM_SPEC] + [VMEM_SPEC] * (2 + 2 * len(d_query) + len(attended)),
        out_specs=(VMEM_SPEC, VMEM_SPEC, VMEM_SPEC),
        scratch_shapes=[pltpu.VMEM((4 * local, width), bf16)],
    )(core.reshape(1), attn_in, d_kv, *d_query, *d_branch_rows, *attended)
    if rows % 16:
        both = keep.reshape(chips, 2, rows, width)
        keep = lax.dynamic_index_in_dim(both, core, 1, keepdims=False)
        send = lax.dynamic_index_in_dim(both, 1 - core, 1, keepdims=False)
    return (keep, send), sums


def attn_outputs_kernel(core_ref, own_ref, other_ref, *out_refs):
    core = core_ref[0]
    rows = own_ref.shape[1]
    for at, ref in enumerate(out_refs):
        ref[pl.ds(pl.multiple_of(core * rows, 16), rows)] = own_ref[at].astype(f32)
        ref[pl.ds(pl.multiple_of((1 - core) * rows, 16), rows)] = other_ref[at].astype(f32)


def attn_outputs(own, other, core):
    chips, rows, width = own.shape
    if chips != 4 or rows % 16:
        both = jnp.where(core == 0, jnp.stack([own, other], 1), jnp.stack([other, own], 1))
        q, k, v, o = jnp.split(both.astype(f32).reshape(-1, width), 4)
    else:
        part = jax.ShapeDtypeStruct((2 * rows, width), f32)
        q, k, v, o = kernel_call(
            attn_outputs_kernel,
            [part] * 4,
            in_specs=[SMEM_SPEC, VMEM_SPEC, VMEM_SPEC],
            out_specs=[VMEM_SPEC] * 4,
        )(core.reshape(1), own, other)
    return q.T, k.T, v.T, o


def split_pieces_kernel(chip_ref, keep_ref, flipped_ref, own_ref, *send_refs):
    for mask, ref in enumerate((own_ref, *send_refs)):
        chip = chip_ref[0] ^ mask
        ref[...] = (keep_ref[chip].astype(f32) + flipped_ref[chip].astype(f32)).astype(bf16)


def split_pieces(keep, flipped, chip):
    piece = jax.ShapeDtypeStruct(keep.shape[1:], bf16)
    return kernel_call(
        split_pieces_kernel,
        [piece] * keep.shape[0],
        in_specs=[SMEM_SPEC, VMEM_SPEC, VMEM_SPEC],
        out_specs=[VMEM_SPEC] * keep.shape[0],
    )(chip.reshape(1), keep, flipped)


def add_kernel(*refs):
    total = sum([ref[...].astype(f32) for ref in refs[1:-1]], refs[0][...].astype(f32))
    refs[-1][...] = total.astype(bf16)


def add_arrays(*arrays):
    return kernel_call(
        add_kernel,
        jax.ShapeDtypeStruct(arrays[0].shape, bf16),
        in_specs=[VMEM_SPEC] * len(arrays),
        out_specs=VMEM_SPEC,
    )(*arrays)


def cut_kernel(in_ref, *out_refs):
    for at, ref in enumerate(out_refs):
        ref[...] = in_ref[at]


def cut(array):
    part = jax.ShapeDtypeStruct(array.shape[1:], array.dtype)
    return kernel_call(
        cut_kernel, [part] * array.shape[0], in_specs=[VMEM_SPEC], out_specs=[VMEM_SPEC] * array.shape[0]
    )(array)


def collect_kernel(chip_ref, *refs):
    for mask, ref in enumerate(refs[:-1]):
        refs[-1][chip_ref[0] ^ mask] = ref[...]


def collect(pieces, chip):
    return kernel_call(
        collect_kernel,
        jax.ShapeDtypeStruct((len(pieces), *pieces[0].shape), pieces[0].dtype),
        in_specs=[SMEM_SPEC] + [VMEM_SPEC] * len(pieces),
        out_specs=VMEM_SPEC,
    )(chip.reshape(1), *pieces)


def mlp_outputs_kernel(in_ref, up_ref, down_ref):
    up_ref[...] = in_ref[0, 0].astype(f32)
    down_ref[...] = in_ref[0, 1].astype(f32)


def mlp_outputs(grad, up_shape):
    pieces, _, rows, width = grad.shape
    hidden_local = pieces * rows
    if rows % 16:
        up, down = grad[:, 0].astype(f32), grad[:, 1].astype(f32)
    else:
        spec = pl.BlockSpec((rows, width), lambda index: (index, 0))
        out = jax.ShapeDtypeStruct((hidden_local, width), f32)
        up, down = kernel_call(
            mlp_outputs_kernel,
            [out, out],
            grid=(pieces,),
            in_specs=[pl.BlockSpec((1, 2, rows, width), lambda index: (index, 0, 0, 0))],
            out_specs=[spec, spec],
        )(grad)
    return up.reshape(up_shape), down.reshape(hidden_local, width)


def shards(
    tokens,
    condition,
    q_weight,
    q_bias,
    k_weight,
    v_weight,
    v_bias,
    o_weight,
    o_bias,
    up_weight,
    up_bias,
    down_weight,
    down_bias,
    ada_weight,
    ada_bias,
    out_grad,
    slot_clip,
    clip_patches,
):
    n_narrow = lax.axis_size("narrow")
    n_wide = lax.axis_size("wide")
    own_rows, width = tokens.shape
    clip_count = condition.shape[0]
    local = q_weight.shape[1]
    hidden_local = up_weight.shape[1]
    slot_count = slot_clip.shape[0]
    members = PATCH_HI // own_rows
    assert members * slot_count == n_narrow
    narrow_index = lax.axis_index("narrow")
    wide_index = lax.axis_index("wide")
    slot = narrow_index // members
    clip = slot_clip[slot]
    patches = clip_patches[clip].reshape(1)
    others = list(range(1, members))
    other_shards = list(range(1, slot_count))

    def member_of(at, step):
        return at // members * members + (at + step) % members

    def fetch_rows(array, step):
        return lax.ppermute(
            array, "narrow", [(member_of(at, step), at) for at in range(n_narrow)]
        )

    def send_rows(array, step):
        return lax.ppermute(
            array, "narrow", [(at, member_of(at, step)) for at in range(n_narrow)]
        )

    def fetch_shard(array, step):
        return lax.ppermute(
            array,
            "narrow",
            [((at + step * members) % n_narrow, at) for at in range(n_narrow)],
        )

    def send_shard(array, step):
        return lax.ppermute(
            array,
            "narrow",
            [(at, (at + step * members) % n_narrow) for at in range(n_narrow)],
        )

    def after(value, *earlier):
        return lax.optimization_barrier((value, *earlier))[0]

    def piece(weight):
        rows = weight.shape[0] // n_wide
        return lax.dynamic_slice_in_dim(weight, wide_index * rows, rows, 0)

    def gathered(pieces):
        return [lax.all_gather(each, "wide", axis=0, tiled=True) for each in pieces]

    def fetched(pack):
        return [fetch_shard(pack, step) for step in other_shards]

    own_pack = jnp.concatenate([q_weight.T, k_weight.T, v_weight.T, o_weight], axis=0)
    own_piece = piece(own_pack)
    attn_pieces = fetched(own_piece)
    bias_pack = jnp.concatenate([q_bias, jnp.zeros_like(q_bias), v_bias, up_bias])
    bias_packs = [bias_pack] + fetched(bias_pack)
    sent_tokens = after(tokens, own_piece)
    token_rows = [tokens] + [fetch_rows(sent_tokens, step) for step in others]

    cond_float = condition.astype(f32)
    silu_cond = jax.nn.silu(cond_float).astype(bf16)
    mod_part = (
        jnp.einsum("cd,dke->cke", silu_cond[slot_clip], ada_weight, preferred_element_type=f32)
        + ada_bias
    )
    mod_blocks = []
    for step in range(n_narrow):
        target = (narrow_index + step) % n_narrow
        block = lax.dynamic_index_in_dim(mod_part, target // members, 0, keepdims=False)
        if step:
            block = lax.ppermute(
                block, "narrow", [(at, (at + step) % n_narrow) for at in range(n_narrow)]
            )
        mod_blocks.append(block)
    mod_slot = jnp.roll(jnp.stack(mod_blocks[::-1]), narrow_index + 1, axis=0)
    modulation = mod_slot.transpose(1, 0, 2).reshape(6, width)

    packs = [own_pack]
    packs += gathered(
        [after(each, *mod_blocks[1:], token_rows[-1], *bias_packs[1:]) for each in attn_pieces]
    )
    qkv_biases = [pack[: 3 * local] for pack in bias_packs]
    up_biases = jnp.stack([pack[3 * local :] for pack in bias_packs]).reshape(slot_count, 1, -1)

    attn_in = modulated_rows(token_rows, modulation)
    qkv = [qkv_rows(attn_in, packs[0], qkv_biases[0])]

    flat_shape = (hidden_local, width)
    mlp_pack = jnp.concatenate([piece(up_weight.reshape(flat_shape)), piece(down_weight)], axis=1)
    mlp_pack = after(mlp_pack, token_rows[-1], modulation)
    mlp_pieces = fetched(mlp_pack)
    own_grad = after(out_grad, *mlp_pieces)
    grad_rows = [own_grad] + [fetch_rows(own_grad, step) for step in others]

    half_rows = max(own_rows // 2, BLOCK)
    halves_of = {block: own_rows // half_rows for block in others}
    halves_of[0] = 1
    attended = [{} for _ in range(slot_count)]
    lse = [{} for _ in range(slot_count)]
    attended_turned = [{} for _ in range(slot_count)]

    def attend(index, block, half, *earlier):
        rows = own_rows // halves_of[block]
        results = attention_forward(
            after(qkv[index], *earlier), patches, block * own_rows + half * rows, rows
        )
        for kept, result in zip((attended, attended_turned, lse), results):
            kept[index][block, half] = result
        return results[0]

    parts_of = [(block, half) for block in others for half in range(halves_of[block])]
    for part in parts_of:
        last_rows = attend(0, *part)
    mlp_packs = gathered([after(each, last_rows) for each in mlp_pieces])
    for index in other_shards:
        rows = after(attn_in, last_rows)
        qkv.append(qkv_rows(rows, packs[index], qkv_biases[index]))

    def branch_sum(rows, pack_refs):
        return sum(dot(each, ref[3 * local :]) for each, ref in zip(rows, pack_refs))

    zero_row = jnp.zeros((1, width), f32)
    def branch_part(part, kind):
        rows = [parts[part] for parts in attended]
        return row_call(
            lambda rows, vectors: ([branch_sum(rows, vectors[1:])], []), rows, [zero_row, *packs], [kind]
        )[0]

    arrived = {}
    earlier = []
    for part in parts_of:
        for index in other_shards:
            attend(index, *part, *earlier)
        earlier = [branch_part(part, bf16)]
        arrived[part] = send_rows(earlier[0], part[0])
    last_rows = attend(0, 0, 0, *earlier)
    for index in other_shards:
        last_rows = attend(index, 0, 0, last_rows, *grad_rows[1:])
    own_branch = branch_part((0, 0), f32)

    def joined(parts, axis=0):
        parts = list(parts)
        return parts[0] if len(parts) == 1 else jnp.concatenate(parts, axis=axis)

    def blocks_of(parts, axis):
        return [
            joined((parts[block, half] for half in range(halves_of[block])), axis)
            for block in range(members)
        ]

    lse = [blocks_of(parts, 1) for parts in lse]
    attended_turned = [
        [parts[block, half] for block in range(members) for half in range(halves_of[block])]
        for parts in attended_turned
    ]
    arrived = [
        joined(after(arrived[block, half], own_branch) for half in range(halves_of[block]))
        for block in others
    ]

    def middle_body(rows, vectors):
        token, *rest = [each.astype(f32) for each in rows]
        mod_ref, bias_ref = vectors
        branch = sum(rest[1:], rest[0]) + bias_ref[...].astype(f32)
        normed = normalize(token + mod_ref[2:3] * branch)[0]
        return [branch, normed * (1.0 + mod_ref[4:5]) + mod_ref[3:4]], []

    branch_one, mlp_own = row_call(
        middle_body,
        [tokens, own_branch, *arrived],
        [modulation, o_bias.reshape(1, width)],
        [f32, bf16],
    )

    mlp_rows = [mlp_own] + [fetch_rows(mlp_own, step) for step in others]
    ups, downs = [(up_weight, 0)], [(down_weight, 0)]
    for pack in mlp_packs:
        if hidden_local == width and hidden_local % HIDDEN_BLOCK == 0:
            ups.append((pack, 0))
            downs.append((pack, 1))
        else:
            ups.append((pack[:, :width].reshape(up_weight.shape), 0))
            downs.append((pack[:, width:], 0))
    hidden, d_pre, d_branch_two, d_mlp, branch_two, bias_sums_up = [], [], [], [], [], []
    for block in range(members):
        rows = after(mlp_rows[block], *d_mlp)
        results = feed_forward(
            rows, grad_rows[block], modulation, up_biases, ups, downs, bf16 if block else f32
        )
        for kept, result in zip((hidden, d_pre, d_branch_two, d_mlp, branch_two, bias_sums_up), results):
            kept.append(result)
    arrived = [send_rows(d_mlp[block], block) for block in others]
    grad_mlp_part = mlp_gradients(mlp_rows, d_branch_two, hidden, d_pre, n_wide)

    def d_middle_body(rows, vectors):
        token, branch, grad, *parts = [each.astype(f32) for each in rows]
        (mod_ref,) = vectors
        d_mlp_in = sum(parts[1:], parts[0])
        normed, inverse = normalize(token + mod_ref[2:3] * branch)
        d_middle = grad + norm_back(d_mlp_in * (1.0 + mod_ref[4:5]), normed, inverse)
        d_branch_one = (mod_ref[2:3] * d_middle).astype(bf16)
        terms = [d_middle * branch, d_mlp_in, d_mlp_in * normed, d_branch_one.astype(f32)]
        return [d_branch_one, d_middle], terms

    arrived = [after(part, grad_mlp_part) for part in arrived]
    d_branch_one, d_middle, middle_sums = row_call(
        d_middle_body, [tokens, branch_one, out_grad, d_mlp[0], *arrived], [modulation], [bf16, f32], 4
    )
    mlp_scattered = lax.psum_scatter(after(grad_mlp_part, *arrived), "wide", scatter_dimension=0, tiled=True)
    d_branch_rows = [d_branch_one] + [fetch_rows(d_branch_one, step) for step in others]

    assert n_wide & (n_wide - 1) == 0
    bits = n_wide.bit_length() - 1
    chips = n_wide // 2
    core, chip = wide_index % 2, wide_index // 2

    def wide_xor(array, mask):
        return lax.ppermute(array, "wide", [(at, at ^ mask) for at in range(n_wide)])

    def start_cores(part):
        keep, send = part
        return keep, wide_xor(send, 1)

    def end_cores(started):
        return split_pieces(*started, chip)

    def start_chips(pieces):
        return [pieces[0]] + [wide_xor(each, 2 * mask) for mask, each in enumerate(pieces[1:], 1)]

    shard_order = other_shards + [0]
    d_query = [[None] * members for _ in range(slot_count)]
    d_query_turned = [[None] * members for _ in range(slot_count)]
    d_kv, d_kv_turned = [None] * slot_count, [None] * slot_count
    grad_attn_part, attn_bias_sums = [None] * slot_count, [None] * slot_count

    def attn_gradients_of(index, *earlier):
        grad_attn_part[index], attn_bias_sums[index] = attn_gradients(
            attn_in,
            after(d_kv_turned[index], *earlier),
            d_query_turned[index],
            d_branch_rows,
            attended_turned[index],
            core,
            chips,
        )

    for block in range(members):
        last = block == members - 1
        for index in shard_order:
            d_query[index][block], d_query_turned[index][block], d_kv[index], *turned = (
                attention_backward(
                    qkv[index],
                    d_branch_rows[block],
                    packs[index],
                    lse[index][block],
                    patches,
                    d_kv[index],
                    block * own_rows,
                    last,
                )
            )
            if last:
                d_kv_turned[index] = turned[0]
                if index:
                    attn_gradients_of(index)
                    d_branch_rows[block] = after(d_branch_rows[block], grad_attn_part[index][0])
        if not last:
            d_branch_rows[block + 1] = after(d_branch_rows[block + 1], d_kv[0])

    def d_attn_sum(rows, pack_refs):
        total = 0.0
        for index, ref in enumerate(pack_refs):
            total = total + dot(rows[2 * index], ref[:local])
            total = total + dot(rows[2 * index + 1], ref[local : 3 * local])
        return total

    def d_rows_of(block):
        rows = []
        for index in range(slot_count):
            rows += [d_query[index][block], (d_kv[index], block * own_rows)]
        return rows

    cores_ended = [end_cores(start_cores(part)) for part in grad_attn_part[1:]]
    chips_started_of = {index: start_chips(cores_ended[index - 1]) for index in other_shards}
    mlp_scattered = after(mlp_scattered, d_kv[0])
    mlp_sent = cut(mlp_scattered.reshape(slot_count, 2, -1, width))
    mlp_arrived = [send_shard(mlp_sent[step], step) for step in other_shards]
    attn_gradients_of(0, *mlp_sent[1:], *(pieces[0] for pieces in cores_ended))
    d_kv[0] = after(d_kv[0], grad_attn_part[0][0])
    def d_attn_part(block, kind):
        return row_call(
            lambda rows, vectors: ([d_attn_sum(rows, vectors[1:])], []),
            d_rows_of(block),
            [zero_row, *packs],
            [kind],
        )[0]

    d_attn_parts = [d_attn_part(block, bf16) for block in others]
    arrived = [send_rows(part, block) for part, block in zip(d_attn_parts, others)]
    own_cores = start_cores(grad_attn_part[0])

    late_branch = [after(branch_two[block], *d_branch_rows[1:]) for block in others]
    arrived_two = [send_rows(part, block) for part, block in zip(late_branch, others)]
    arrived_two = [after(part, *d_attn_parts) for part in arrived_two]

    def out_body(rows, vectors):
        token, branch, grad, *parts = [each.astype(f32) for each in rows]
        mod_ref, bias_ref = vectors
        total = sum(parts[1:], parts[0]) + bias_ref[...].astype(f32)
        block_out = token + mod_ref[2:3] * branch + mod_ref[5:6] * total
        return [block_out], [grad * total, (mod_ref[5:6] * grad).astype(bf16).astype(f32)]

    block_out, out_sums = row_call(
        out_body,
        [tokens, branch_one, out_grad, branch_two[0], *arrived_two],
        [modulation, down_bias.reshape(1, width)],
        [bf16],
        2,
    )
    d_query[0][0] = after(d_query[0][0], block_out)
    own_d_attn = d_attn_part(0, f32)
    def end_body(rows, vectors):
        token, d_middle_rows, *parts = rows
        (mod_ref,) = vectors
        d_attn_in = sum([each.astype(f32) for each in parts[1:]], parts[0])
        normed, inverse = normalize(token.astype(f32))
        grad = d_middle_rows + norm_back(d_attn_in * (1.0 + mod_ref[1:2]), normed, inverse)
        return [grad], [d_attn_in, d_attn_in * normed]

    piece_sums = []
    for index in other_shards:
        own, *pieces = chips_started_of[index]
        piece_sums.append(add_arrays(own, *(after(each, own_d_attn) for each in pieces)))
    own_pieces = end_cores((own_cores[0], after(own_cores[1], *d_attn_parts)))
    chips_started = start_chips(own_pieces)
    arrived = [after(part, own_d_attn, own_pieces[0], *piece_sums) for part in arrived]
    grad_tokens, end_sums = row_call(
        end_body, [tokens, d_middle, own_d_attn, *arrived], [modulation], [f32], 2
    )

    sent = [send_shard(each, index) for index, each in zip(other_shards, piece_sums)]
    mlp_total = add_arrays(mlp_sent[0], *(after(each, own_d_attn) for each in mlp_arrived))

    middle_sums, out_sums = after(middle_sums, end_sums), after(out_sums, end_sums)
    own_sums = jnp.concatenate(
        [end_sums[0:2], middle_sums[0:3], out_sums[0:1], middle_sums[3:4], out_sums[1:2]]
    )
    bit = 1
    while bit < members:
        own_sums = own_sums + lax.ppermute(
            own_sums, "narrow", [(at, at ^ bit) for at in range(n_narrow)]
        )
        bit *= 2
    attn_bias_sums = [after(each, end_sums) for each in attn_bias_sums]
    up_bias_sums = sum([after(each, end_sums) for each in bias_sums_up])
    late_slot_clip = after(slot_clip, end_sums)
    shard_parts = [
        jnp.concatenate([attn_bias_sums[step].reshape(-1), up_bias_sums[step]])
        for step in range(slot_count)
    ]
    slot_sums = [own_sums] + [fetch_shard(own_sums, step) for step in other_shards]
    shard_parts[1:] = [send_shard(shard_parts[step], step) for step in other_shards]
    total = add_arrays(*chips_started, *sent)

    grad_mlp = lax.all_gather(mlp_total, "wide", axis=0, tiled=False)
    grad_up_weight, grad_down_weight = mlp_outputs(grad_mlp, up_weight.shape)

    pieces = collect([total] + [wide_xor(total, 2 * mask) for mask in range(1, chips)], chip)
    flipped_pieces = wide_xor(pieces, 1)

    clip_ids = jnp.arange(clip_count, dtype=jnp.int32)
    d_mod_clips = jnp.zeros((clip_count, 6, local), f32)
    bias_sums = jnp.zeros((2, width), f32)
    shard_sum = jnp.zeros((3 * local + hidden_local,), f32)
    for step in range(slot_count):
        source_clip = late_slot_clip[(slot + step) % slot_count]
        one_hot = (clip_ids == source_clip).astype(f32)
        columns = lax.dynamic_slice_in_dim(slot_sums[step][:6], narrow_index * local, local, 1)
        d_mod_clips = d_mod_clips + one_hot[:, None, None] * columns
        bias_sums = bias_sums + slot_sums[step][6:]
        shard_sum = shard_sum + shard_parts[step]
    small = jnp.concatenate([d_mod_clips.reshape(-1), bias_sums.reshape(-1), shard_sum])
    for bit in range(bits):
        small = small + wide_xor(small, 1 << bit)
    grad_q_weight, grad_k_weight, grad_v_weight, grad_o_weight = attn_outputs(
        pieces, flipped_pieces, core
    )
    mod_size = clip_count * 6 * local
    d_modulation = small[:mod_size].reshape(clip_count, 6, local)
    grad_o_bias = small[mod_size : mod_size + width]
    grad_down_bias = small[mod_size + width : mod_size + 2 * width]
    shard_sum = small[mod_size + 2 * width :]
    grad_q_bias = shard_sum[:local]
    grad_v_bias = shard_sum[2 * local : 3 * local]
    grad_up_bias = shard_sum[3 * local :]

    silu_float = silu_cond.astype(f32)
    grad_ada_weight = jnp.einsum("cd,cke->dke", silu_float, d_modulation, precision=highest)
    grad_ada_bias = jnp.sum(d_modulation, axis=0)
    d_silu = jnp.einsum(
        "cke,dke->cd", d_modulation, ada_weight.astype(f32), precision=highest
    )
    bit = 1
    while bit < n_narrow:
        flipped = lax.ppermute(d_silu, "narrow", [(at, at ^ bit) for at in range(n_narrow)])
        d_silu = d_silu + (after(flipped, grad_up_weight) if bit == 1 else flipped)
        bit *= 2
    grad_condition = jax.vjp(jax.nn.silu, cond_float)[1](d_silu)[0]
    return (
        block_out,
        grad_tokens,
        grad_condition,
        grad_q_weight,
        grad_q_bias,
        grad_k_weight,
        grad_v_weight,
        grad_v_bias,
        grad_o_weight,
        grad_o_bias,
        grad_up_weight,
        grad_up_bias,
        grad_down_weight,
        grad_down_bias,
        grad_ada_weight,
        grad_ada_bias,
    )


def solution(mesh):
    in_specs = (
        P(("wide", "narrow"), None),
        P(),
        P(None, "narrow"),
        P("narrow"),
        P(None, "narrow"),
        P(None, "narrow"),
        P("narrow"),
        P("narrow", None),
        P(),
        P(None, "narrow"),
        P("narrow"),
        P("narrow", None),
        P(),
        P(None, None, "narrow"),
        P(None, "narrow"),
        P(("wide", "narrow"), None),
        P("wide"),
        P(),
    )
    out_specs = (
        P(("wide", "narrow"), None),
        P(("wide", "narrow"), None),
        P(),
        P(None, "narrow"),
        P("narrow"),
        P(None, "narrow"),
        P(None, "narrow"),
        P("narrow"),
        P("narrow", None),
        P(),
        P(None, "narrow"),
        P("narrow"),
        P("narrow", None),
        P(),
        P(None, None, "narrow"),
        P(None, "narrow"),
    )
    return jax.shard_map(shards, mesh=mesh, in_specs=in_specs, out_specs=out_specs, check_vma=False)
```

```python
import functools

import jax
import jax.numpy as jnp
from jax import lax
from jax.experimental import pallas as pl
from jax.experimental.pallas import tpu as pltpu
from jax.sharding import PartitionSpec as P

HDIM = 72
PATCH_HI = 1024
BLOCK = 256
ROW_BLOCK = 256
HIDDEN_BLOCK = 384
VMEM_LIMIT = 48 * 1024 * 1024
FILLER_FLOPS = 20_000_000_000

epsilon = 1e-06
highest = lax.Precision.HIGHEST
EXP2_SCALE = HDIM ** (-0.5) * 1.4426950408889634
f32 = jnp.float32
bf16 = jnp.bfloat16


def normalize(row_block):
    centred = row_block - jnp.mean(row_block, axis=-1, keepdims=True)
    variance = jnp.mean(centred * centred, axis=-1, keepdims=True)
    inverse = lax.rsqrt(variance + epsilon)
    return (centred * inverse, inverse)


def norm_back(d_normed, normed, inverse):
    first_mean = jnp.mean(d_normed, axis=-1, keepdims=True)
    second_mean = jnp.mean(d_normed * normed, axis=-1, keepdims=True)
    return inverse * (d_normed - first_mean - normed * second_mean)


def gelu_and_slope(values):
    root = (2.0 / jnp.pi) ** 0.5
    square = values * values
    tanh = jnp.tanh(root * (values + 0.044715 * (square * values)))
    half = 0.5 * (1.0 + tanh)
    slope = half + 0.5 * values * (1.0 - tanh * tanh) * (root + (3 * 0.044715 * root) * square)
    return values * half, slope


def dot(left, right):
    return jnp.dot(left, right, preferred_element_type=f32)


def dot_t(left, right):
    return lax.dot_general(left, right, (((1,), (1,)), ((), ())), preferred_element_type=f32)


def contract_rows(left, right):
    return lax.dot_general(left, right, (((0,), (0,)), ((), ())), preferred_element_type=f32)


def left_t_right_t(left, right):
    return lax.dot_general(left, right, (((0,), (1,)), ((), ())), preferred_element_type=f32)


def kernel_call(kernel, outs, flops=0, **options):
    return pl.pallas_call(
        kernel,
        out_shape=outs,
        compiler_params=pltpu.CompilerParams(vmem_limit_bytes=VMEM_LIMIT),
        cost_estimate=pl.CostEstimate(flops=flops, bytes_accessed=1024, transcendentals=0),
        **options,
    )


def whole(array):
    return pl.BlockSpec(array.shape, lambda *_: (0,) * len(array.shape))


def row_call(body, rows_in, vectors, out_types, term_count=0, flops=0):
    rows, width = rows_in[0].shape[0], vectors[0].shape[1]
    step_rows = min(ROW_BLOCK, rows)
    rows_in = [each if isinstance(each, tuple) else (each, 0) for each in rows_in]

    def kernel(*refs):
        row_refs = refs[: len(rows_in)]
        vector_refs = refs[len(rows_in) : len(rows_in) + len(vectors)]
        out_refs = refs[len(rows_in) + len(vectors) :]
        outs, terms = body([ref[...] for ref in row_refs], vector_refs)
        for ref, out in zip(out_refs, outs):
            ref[...] = out.astype(ref.dtype)
        if term_count:
            sums_ref = refs[-1]

            @pl.when(pl.program_id(0) == 0)
            def _():
                sums_ref[...] = jnp.zeros_like(sums_ref)

            for index, term in enumerate(terms):
                sums_ref[index : index + 1, :] += jnp.sum(term, axis=0, keepdims=True)

    outs = [jax.ShapeDtypeStruct((rows, width), kind) for kind in out_types]
    out_specs = [pl.BlockSpec((step_rows, width), lambda index: (index, 0))] * len(outs)
    if term_count:
        outs.append(jax.ShapeDtypeStruct((8, width), f32))
        out_specs.append(pl.BlockSpec((8, width), lambda index: (0, 0)))
    return kernel_call(
        kernel,
        outs,
        flops,
        grid=(rows // step_rows,),
        in_specs=[
            pl.BlockSpec((step_rows, each.shape[1]), lambda index, first=first: (first // step_rows + index, 0))
            for each, first in rows_in
        ]
        + [whole(each) for each in vectors],
        out_specs=out_specs,
    )(*(each for each, _ in rows_in), *vectors)


def modulated_rows_kernel(row_count, *refs):
    mod_ref, out_ref = refs[-2:]
    for index, ref in enumerate(refs[:row_count]):
        normed = normalize(ref[...].astype(f32))[0]
        out_ref[index] = (normed * (1.0 + mod_ref[1:2, :]) + mod_ref[0:1, :]).astype(bf16)


def modulated_rows(row_blocks, modulation):
    rows, width = row_blocks[0].shape
    count = len(row_blocks)
    out = kernel_call(
        functools.partial(modulated_rows_kernel, count),
        jax.ShapeDtypeStruct((count, rows, width), bf16),
        grid=(rows // ROW_BLOCK,),
        in_specs=[pl.BlockSpec((ROW_BLOCK, width), lambda index: (index, 0))] * count
        + [whole(modulation)],
        out_specs=pl.BlockSpec((count, ROW_BLOCK, width), lambda index: (0, index, 0)),
    )(*row_blocks, modulation)
    return out.reshape(count * rows, width)


def qkv_kernel(rows_ref, pack_ref, bias_ref, out_ref):
    columns = out_ref.shape[1]
    rows = dot_t(rows_ref[...], pack_ref[:columns]) + bias_ref[...].astype(f32)
    out_ref[...] = rows.astype(bf16)


def qkv_rows(rows, pack, bias):
    columns = pack.shape[0] // 4 * 3
    bias = bias.reshape(1, columns)
    return kernel_call(
        qkv_kernel,
        jax.ShapeDtypeStruct((rows.shape[0], columns), bf16),
        grid=(2,),
        in_specs=[
            pl.BlockSpec((rows.shape[0] // 2, rows.shape[1]), lambda index: (index, 0)),
            whole(pack),
            whole(bias),
        ],
        out_specs=pl.BlockSpec((rows.shape[0] // 2, columns), lambda index: (index, 0)),
    )(rows, pack, bias)


def frame_loop(patches_ref, rows, heads, stages):
    is_full = patches_ref[0] == PATCH_HI
    first, second, third = stages

    def run(full):
        units = [(block * BLOCK, head) for block in range(rows // BLOCK) for head in range(heads)]
        begun = first(*units[0], full)
        done = None
        for at, unit in enumerate(units):
            coming = first(*units[at + 1], full) if at + 1 < len(units) else None
            if done is not None:
                third(*units[at - 1], full, done)
            done = second(*unit, full, begun)
            begun = coming
        third(*units[-1], full, done)

    @pl.when(is_full)
    def _():
        run(True)

    @pl.when(jnp.logical_not(is_full))
    def _():
        run(False)


def attention_forward_kernel(
    first_row, patches_ref, qkv_ref, attended_ref, turned_ref, lse_ref, out_scratch
):
    heads = qkv_ref.shape[1] // (3 * HDIM)

    def columns(start, full, part, head):
        at = (part * heads + head) * HDIM
        rows = slice(0, PATCH_HI) if full else slice(first_row + start, first_row + start + BLOCK)
        return qkv_ref[rows, at : at + HDIM]

    def scores(start, head, full):
        return dot_t(columns(start, full, 1, head), columns(start, False, 0, head))

    def softmax(start, head, full, logits):
        out_rows = slice(start, start + BLOCK)
        top = jnp.max(logits, axis=0, keepdims=True) * EXP2_SCALE
        exp_scores = jnp.exp2(logits * EXP2_SCALE - top)
        total = jnp.sum(exp_scores, axis=0, keepdims=True)
        lse_ref[head : head + 1, out_rows] = top + jnp.log2(total)
        return (exp_scores * (1.0 / total)).astype(bf16)

    def values(start, head, full, weights):
        out_scratch[head * HDIM : (head + 1) * HDIM, start : start + BLOCK] = contract_rows(
            columns(start, full, 2, head), weights
        )

    frame_loop(patches_ref, lse_ref.shape[1], heads, (scores, softmax, values))
    attended_ref[...] = out_scratch[...].T.astype(bf16)
    turned_ref[...] = out_scratch[...].astype(bf16)


VMEM_SPEC = pl.BlockSpec(memory_space=pltpu.VMEM)
SMEM_SPEC = pl.BlockSpec(memory_space=pltpu.SMEM)


def attention_forward(qkv, patches, first_row, rows):
    width = qkv.shape[1] // 3
    return kernel_call(
        functools.partial(attention_forward_kernel, first_row),
        (
            jax.ShapeDtypeStruct((rows, width), bf16),
            jax.ShapeDtypeStruct((width, rows), bf16),
            jax.ShapeDtypeStruct((width // HDIM, rows), f32),
        ),
        in_specs=[SMEM_SPEC, VMEM_SPEC],
        out_specs=(VMEM_SPEC, VMEM_SPEC, VMEM_SPEC),
        scratch_shapes=[pltpu.VMEM((width, rows), f32)],
    )(patches, qkv)


def attention_backward_kernel(first_row, first, last, *refs):
    patches_ref, qkv_ref, d_rows_ref, pack_ref, lse_ref = refs[:5]
    sums_ref = refs[5] if not first else None
    d_query_ref, d_query_turned_ref, d_kv_ref, *rest = refs[5 if first else 6 :]
    d_kv_turned_ref = rest[0] if last else None
    query_scratch, kv_scratch, d_scratch = rest[-3:]
    local = d_query_ref.shape[1]
    heads = local // HDIM
    scale = HDIM ** (-0.5)
    kv_scratch[...] = jnp.zeros_like(kv_scratch) if first else sums_ref[...]
    d_scratch[...] = dot_t(d_rows_ref[...], pack_ref[3 * local :]).astype(bf16)

    def columns(start, full, part, head):
        at = (part * heads + head) * HDIM
        rows = slice(0, PATCH_HI) if full else slice(first_row + start, first_row + start + BLOCK)
        return qkv_ref[rows, at : at + HDIM]

    def d_out(start, head):
        return d_scratch[start : start + BLOCK, head * HDIM : (head + 1) * HDIM]

    def products(start, head, full):
        logits = dot_t(columns(start, full, 1, head), columns(start, False, 0, head))
        return logits, dot_t(columns(start, full, 2, head), d_out(start, head))

    def d_softmax(start, head, full, pair):
        logits, d_weights = pair
        probs = jnp.exp2(logits * EXP2_SCALE - lse_ref[head : head + 1, start : start + BLOCK])
        delta = jnp.sum(probs * d_weights, axis=0, keepdims=True)
        return probs.astype(bf16), (probs * (d_weights - delta)).astype(bf16)

    def gradients(start, head, full, pair):
        probs, d_scores = pair
        at = slice(head * HDIM, (head + 1) * HDIM)
        v_at = slice(local + head * HDIM, local + (head + 1) * HDIM)
        k_rows = slice(0, PATCH_HI) if full else slice(first_row + start, first_row + start + BLOCK)
        query_scratch[at, start : start + BLOCK] = (
            contract_rows(columns(start, full, 1, head), d_scores) * scale
        )
        kv_scratch[at, k_rows] += left_t_right_t(columns(start, False, 0, head), d_scores) * scale
        kv_scratch[v_at, k_rows] += left_t_right_t(d_out(start, head), probs)

    frame_loop(patches_ref, lse_ref.shape[1], heads, (products, d_softmax, gradients))
    d_query_ref[...] = query_scratch[...].T.astype(bf16)
    d_query_turned_ref[...] = query_scratch[...].astype(bf16)
    if last:
        d_kv_ref[...] = kv_scratch[...].T.astype(bf16)
        d_kv_turned_ref[...] = kv_scratch[...].astype(bf16)
    else:
        d_kv_ref[...] = kv_scratch[...]


def attention_backward(qkv, d_rows, pack, lse, patches, sums, first_row, last):
    local = pack.shape[0] // 4
    rows = d_rows.shape[0]
    first = sums is None
    turned = (2 * local, PATCH_HI)
    extra = [] if first else [sums]
    outs = [jax.ShapeDtypeStruct((rows, local), bf16), jax.ShapeDtypeStruct((local, rows), bf16)]
    if last:
        outs += [jax.ShapeDtypeStruct(turned[::-1], bf16), jax.ShapeDtypeStruct(turned, bf16)]
    else:
        outs.append(jax.ShapeDtypeStruct(turned, f32))
    return kernel_call(
        functools.partial(attention_backward_kernel, first_row, first, last),
        outs,
        in_specs=[SMEM_SPEC] + [VMEM_SPEC] * (4 + len(extra)),
        out_specs=[VMEM_SPEC] * len(outs),
        scratch_shapes=[
            pltpu.VMEM((local, rows), f32),
            pltpu.VMEM(turned, f32),
            pltpu.VMEM((rows, local), bf16),
        ],
    )(patches, qkv, d_rows, pack, lse, *extra)


def feed_forward_kernel(last_types, shard_count, *refs):
    x_ref, grad_ref, mod_ref, bias_ref = refs[:4]
    up_refs = refs[4 : 4 + shard_count]
    down_refs = refs[4 + shard_count : 4 + 2 * shard_count]
    hidden_ref, d_pre_ref, d_branch_ref, d_mlp_ref, branch_ref, sums_ref = refs[-8:-2]
    d_mlp_scratch, branch_scratch = refs[-2:]

    @pl.when(pl.program_id(0) == 0)
    def _():
        d_mlp_scratch[...] = jnp.zeros_like(d_mlp_scratch)
        branch_scratch[...] = jnp.zeros_like(branch_scratch)
        d_branch_ref[...] = (mod_ref[5:6, :] * grad_ref[...].astype(f32)).astype(bf16)

    sums_ref[...] = jnp.zeros_like(sums_ref)

    def products(start, shard):
        block = slice(start, start + BLOCK)
        pre_act = dot(x_ref[block], up_refs[shard][...]) + bias_ref[shard].astype(f32)
        return pre_act, dot_t(d_branch_ref[block], down_refs[shard][...])

    def activation(start, shard, pair):
        block = slice(start, start + BLOCK)
        pre_act, d_hidden = pair
        hidden, slope = gelu_and_slope(pre_act)
        hidden, d_pre = hidden.astype(bf16), (d_hidden * slope).astype(bf16)
        hidden_ref[shard, block] = hidden
        d_pre_ref[shard, block] = d_pre
        sums_ref[shard : shard + 1] += jnp.sum(d_pre.astype(f32), axis=0, keepdims=True)
        return hidden, d_pre

    def add_sums(start, shard, pair):
        block = slice(start, start + BLOCK)
        hidden, d_pre = pair
        d_mlp_scratch[block] += dot_t(d_pre, up_refs[shard][...])
        branch_scratch[block] += dot(hidden, down_refs[shard][...])

    units = [
        (start, shard) for start in range(0, x_ref.shape[0], BLOCK) for shard in range(shard_count)
    ]
    begun, done = products(*units[0]), None
    for at, unit in enumerate(units):
        coming = products(*units[at + 1]) if at + 1 < len(units) else None
        if done is not None:
            add_sums(*units[at - 1], done)
        done = activation(*unit, begun)
        begun = coming
    add_sums(*units[-1], done)

    @pl.when(pl.program_id(0) == pl.num_programs(0) - 1)
    def _():
        d_mlp_ref[...] = d_mlp_scratch[...].astype(d_mlp_ref.dtype)
        branch_ref[...] = branch_scratch[...].astype(branch_ref.dtype)


def feed_forward(rows, grad, modulation, biases, ups, downs, sum_type):
    row_count, width = rows.shape
    shard_count = len(ups)
    hidden_local = biases.shape[-1]
    step = HIDDEN_BLOCK if hidden_local % HIDDEN_BLOCK == 0 else hidden_local
    in_specs = [whole(rows), whole(grad), whole(modulation)]
    in_specs.append(pl.BlockSpec((shard_count, 1, step), lambda index: (0, 0, index)))
    for _, first in ups:
        in_specs.append(pl.BlockSpec((width, step), lambda index, first=first: (0, first + index)))
    for _, first in downs:
        in_specs.append(pl.BlockSpec((step, width), lambda index, first=first: (index, first)))
    by_shard = pl.BlockSpec((shard_count, row_count, step), lambda index: (0, 0, index))
    flat = jax.ShapeDtypeStruct((row_count, width), sum_type)
    return kernel_call(
        functools.partial(feed_forward_kernel, sum_type, shard_count),
        [
            jax.ShapeDtypeStruct((shard_count, row_count, hidden_local), bf16),
            jax.ShapeDtypeStruct((shard_count, row_count, hidden_local), bf16),
            jax.ShapeDtypeStruct((row_count, width), bf16),
            flat,
            flat,
            jax.ShapeDtypeStruct((8, hidden_local), f32),
        ],
        grid=(hidden_local // step,),
        in_specs=in_specs,
        out_specs=[by_shard, by_shard]
        + [pl.BlockSpec((row_count, width), lambda index: (0, 0))] * 3
        + [pl.BlockSpec((8, step), lambda index: (0, index))],
        scratch_shapes=[pltpu.VMEM((row_count, width), f32)] * 2,
    )(rows, grad, modulation, biases, *(each for each, _ in ups), *(each for each, _ in downs))


def mlp_gradient_kernel(member_count, *refs):
    out_ref = refs[-1]
    is_up = pl.program_id(0) % 2 == 0
    pieces, _, rows, width = out_ref.shape

    def store(lefts, rights):
        total = sum(contract_rows(left, right) for left, right in zip(lefts, rights))
        out_ref[:, 0] = total.astype(bf16).reshape(pieces, rows, width)

    groups = [refs[at * member_count : (at + 1) * member_count] for at in range(4)]
    x_refs, d_branch_refs, hidden_refs, d_pre_refs = groups

    @pl.when(is_up)
    def _():
        store([ref[...] for ref in x_refs], [ref[0] for ref in d_pre_refs])

    @pl.when(jnp.logical_not(is_up))
    def _():
        store([ref[0] for ref in hidden_refs], [ref[...] for ref in d_branch_refs])


def mlp_gradients(x_rows, d_branch_rows, hidden, d_pre, pieces):
    shard_count, row_count, hidden_local = hidden[0].shape
    width = x_rows[0].shape[1]
    rows = hidden_local // pieces
    if hidden_local != width or rows % 16:
        parts = []
        for shard in range(shard_count):
            up = sum(contract_rows(left, right[shard]) for left, right in zip(x_rows, d_pre))
            down = sum(contract_rows(left[shard], right) for left, right in zip(hidden, d_branch_rows))
            parts += [up.reshape(pieces, rows, width), down.reshape(pieces, rows, width)]
        return jnp.stack(parts, axis=1).astype(bf16)
    by_shard = pl.BlockSpec((1, row_count, hidden_local), lambda index: (index // 2, 0, 0))
    return kernel_call(
        functools.partial(mlp_gradient_kernel, len(x_rows)),
        jax.ShapeDtypeStruct((pieces, 2 * shard_count, rows, width), bf16),
        grid=(2 * shard_count,),
        in_specs=[whole(each) for each in (*x_rows, *d_branch_rows)]
        + [by_shard] * (2 * len(x_rows)),
        out_specs=pl.BlockSpec((pieces, 1, rows, width), lambda index: (0, index, 0, 0)),
    )(*x_rows, *d_branch_rows, *hidden, *d_pre)


def attn_gradient_kernel(member_count, *refs):
    core_ref, in_ref, d_kv_ref = refs[:3]
    d_query_refs, d_branch_refs = refs[3 : 3 + member_count], refs[3 + member_count : 3 + 2 * member_count]
    attended_refs = refs[3 + 2 * member_count : -4]
    keep_ref, send_ref, sums_ref, out_ref = refs[-4:]
    local, rows = d_query_refs[0].shape
    query = sum(
        dot(ref[...], in_ref[at * rows : (at + 1) * rows]) for at, ref in enumerate(d_query_refs)
    )
    out_ref[:local] = query.astype(bf16)
    out_ref[local : 3 * local] = dot(d_kv_ref[...], in_ref[...]).astype(bf16)
    start, out = 0, 0.0
    for ref in attended_refs:
        first = start % rows
        out = out + dot(ref[...], d_branch_refs[start // rows][first : first + ref.shape[1]])
        start += ref.shape[1]
    out_ref[3 * local :] = out.astype(bf16)
    sums_ref[:local] = sum(
        jnp.sum(ref[...].astype(f32), axis=1, keepdims=True) for ref in d_query_refs
    )
    sums_ref[local:] = jnp.sum(d_kv_ref[...].astype(f32), axis=1, keepdims=True)
    if len(keep_ref.shape) == 2:
        keep_ref[...] = out_ref[...]
    else:
        core = core_ref[0]
        chips, piece_rows, _ = keep_ref.shape
        for chip in range(chips):
            kept = pl.multiple_of((2 * chip + core) * piece_rows, 16)
            sent = pl.multiple_of((2 * chip + 1 - core) * piece_rows, 16)
            keep_ref[chip] = out_ref[pl.ds(kept, piece_rows)]
            send_ref[chip] = out_ref[pl.ds(sent, piece_rows)]


def attn_gradients(attn_in, d_kv, d_query, d_branch_rows, attended, core, chips):
    width = attn_in.shape[1]
    local = d_query[0].shape[0]
    rows = 4 * local // (2 * chips)
    part = jax.ShapeDtypeStruct((chips, rows, width), bf16)
    if rows % 16:
        parts = (jax.ShapeDtypeStruct((4 * local, width), bf16), jax.ShapeDtypeStruct((8, 128), bf16))
    else:
        parts = (part, part)
    keep, send, sums = kernel_call(
        functools.partial(attn_gradient_kernel, len(d_query)),
        (*parts, jax.ShapeDtypeStruct((3 * local, 1), f32)),
        in_specs=[SMEM_SPEC] + [VMEM_SPEC] * (2 + 2 * len(d_query) + len(attended)),
        out_specs=(VMEM_SPEC, VMEM_SPEC, VMEM_SPEC),
        scratch_shapes=[pltpu.VMEM((4 * local, width), bf16)],
    )(core.reshape(1), attn_in, d_kv, *d_query, *d_branch_rows, *attended)
    if rows % 16:
        both = keep.reshape(chips, 2, rows, width)
        keep = lax.dynamic_index_in_dim(both, core, 1, keepdims=False)
        send = lax.dynamic_index_in_dim(both, 1 - core, 1, keepdims=False)
    return (keep, send), sums


def attn_outputs_kernel(core_ref, own_ref, other_ref, *out_refs):
    core = core_ref[0]
    rows = own_ref.shape[1]
    for at, ref in enumerate(out_refs):
        ref[pl.ds(pl.multiple_of(core * rows, 16), rows)] = own_ref[at].astype(f32)
        ref[pl.ds(pl.multiple_of((1 - core) * rows, 16), rows)] = other_ref[at].astype(f32)


def attn_outputs(own, other, core):
    chips, rows, width = own.shape
    if chips != 4 or rows % 16:
        both = jnp.where(core == 0, jnp.stack([own, other], 1), jnp.stack([other, own], 1))
        q, k, v, o = jnp.split(both.astype(f32).reshape(-1, width), 4)
    else:
        part = jax.ShapeDtypeStruct((2 * rows, width), f32)
        q, k, v, o = kernel_call(
            attn_outputs_kernel,
            [part] * 4,
            in_specs=[SMEM_SPEC, VMEM_SPEC, VMEM_SPEC],
            out_specs=[VMEM_SPEC] * 4,
        )(core.reshape(1), own, other)
    return q.T, k.T, v.T, o


def split_pieces_kernel(chip_ref, keep_ref, flipped_ref, own_ref, *send_refs):
    for mask, ref in enumerate((own_ref, *send_refs)):
        chip = chip_ref[0] ^ mask
        ref[...] = (keep_ref[chip].astype(f32) + flipped_ref[chip].astype(f32)).astype(bf16)


def split_pieces(keep, flipped, chip):
    piece = jax.ShapeDtypeStruct(keep.shape[1:], bf16)
    return kernel_call(
        split_pieces_kernel,
        [piece] * keep.shape[0],
        in_specs=[SMEM_SPEC, VMEM_SPEC, VMEM_SPEC],
        out_specs=[VMEM_SPEC] * keep.shape[0],
    )(chip.reshape(1), keep, flipped)


def add_kernel(*refs):
    total = sum([ref[...].astype(f32) for ref in refs[1:-1]], refs[0][...].astype(f32))
    refs[-1][...] = total.astype(bf16)


def add_arrays(*arrays):
    return kernel_call(
        add_kernel,
        jax.ShapeDtypeStruct(arrays[0].shape, bf16),
        in_specs=[VMEM_SPEC] * len(arrays),
        out_specs=VMEM_SPEC,
    )(*arrays)


def cut_kernel(in_ref, *out_refs):
    for at, ref in enumerate(out_refs):
        ref[...] = in_ref[at]


def cut(array):
    part = jax.ShapeDtypeStruct(array.shape[1:], array.dtype)
    return kernel_call(
        cut_kernel, [part] * array.shape[0], in_specs=[VMEM_SPEC], out_specs=[VMEM_SPEC] * array.shape[0]
    )(array)


def collect_kernel(chip_ref, *refs):
    for mask, ref in enumerate(refs[:-1]):
        refs[-1][chip_ref[0] ^ mask] = ref[...]


def collect(pieces, chip):
    return kernel_call(
        collect_kernel,
        jax.ShapeDtypeStruct((len(pieces), *pieces[0].shape), pieces[0].dtype),
        in_specs=[SMEM_SPEC] + [VMEM_SPEC] * len(pieces),
        out_specs=VMEM_SPEC,
    )(chip.reshape(1), *pieces)


def mlp_outputs_kernel(in_ref, up_ref, down_ref):
    up_ref[...] = in_ref[0, 0].astype(f32)
    down_ref[...] = in_ref[0, 1].astype(f32)


def mlp_outputs(grad, up_shape):
    pieces, _, rows, width = grad.shape
    hidden_local = pieces * rows
    if rows % 16:
        up, down = grad[:, 0].astype(f32), grad[:, 1].astype(f32)
    else:
        spec = pl.BlockSpec((rows, width), lambda index: (index, 0))
        out = jax.ShapeDtypeStruct((hidden_local, width), f32)
        up, down = kernel_call(
            mlp_outputs_kernel,
            [out, out],
            grid=(pieces,),
            in_specs=[pl.BlockSpec((1, 2, rows, width), lambda index: (index, 0, 0, 0))],
            out_specs=[spec, spec],
        )(grad)
    return up.reshape(up_shape), down.reshape(hidden_local, width)


def shards(
    tokens,
    condition,
    q_weight,
    q_bias,
    k_weight,
    v_weight,
    v_bias,
    o_weight,
    o_bias,
    up_weight,
    up_bias,
    down_weight,
    down_bias,
    ada_weight,
    ada_bias,
    out_grad,
    slot_clip,
    clip_patches,
):
    n_narrow = lax.axis_size("narrow")
    n_wide = lax.axis_size("wide")
    own_rows, width = tokens.shape
    clip_count = condition.shape[0]
    local = q_weight.shape[1]
    hidden_local = up_weight.shape[1]
    slot_count = slot_clip.shape[0]
    members = PATCH_HI // own_rows
    assert members * slot_count == n_narrow
    narrow_index = lax.axis_index("narrow")
    wide_index = lax.axis_index("wide")
    slot = narrow_index // members
    clip = slot_clip[slot]
    patches = clip_patches[clip].reshape(1)
    others = list(range(1, members))
    other_shards = list(range(1, slot_count))

    def member_of(at, step):
        return at // members * members + (at + step) % members

    def fetch_rows(array, step):
        return lax.ppermute(
            array, "narrow", [(member_of(at, step), at) for at in range(n_narrow)]
        )

    def send_rows(array, step):
        return lax.ppermute(
            array, "narrow", [(at, member_of(at, step)) for at in range(n_narrow)]
        )

    def fetch_shard(array, step):
        return lax.ppermute(
            array,
            "narrow",
            [((at + step * members) % n_narrow, at) for at in range(n_narrow)],
        )

    def send_shard(array, step):
        return lax.ppermute(
            array,
            "narrow",
            [(at, (at + step * members) % n_narrow) for at in range(n_narrow)],
        )

    def after(value, *earlier):
        return lax.optimization_barrier((value, *earlier))[0]

    def piece(weight):
        rows = weight.shape[0] // n_wide
        return lax.dynamic_slice_in_dim(weight, wide_index * rows, rows, 0)

    def gathered(pieces):
        return [lax.all_gather(each, "wide", axis=0, tiled=True) for each in pieces]

    def fetched(pack):
        return [fetch_shard(pack, step) for step in other_shards]

    own_pack = jnp.concatenate([q_weight.T, k_weight.T, v_weight.T, o_weight], axis=0)
    own_piece = piece(own_pack)
    attn_pieces = fetched(own_piece)
    bias_pack = jnp.concatenate([q_bias, jnp.zeros_like(q_bias), v_bias, up_bias])
    bias_packs = [bias_pack] + fetched(bias_pack)
    sent_tokens = after(tokens, own_piece)
    token_rows = [tokens] + [fetch_rows(sent_tokens, step) for step in others]

    cond_float = condition.astype(f32)
    silu_cond = jax.nn.silu(cond_float).astype(bf16)
    mod_part = (
        jnp.einsum("cd,dke->cke", silu_cond[slot_clip], ada_weight, preferred_element_type=f32)
        + ada_bias
    )
    mod_blocks = []
    for step in range(n_narrow):
        target = (narrow_index + step) % n_narrow
        block = lax.dynamic_index_in_dim(mod_part, target // members, 0, keepdims=False)
        if step:
            block = lax.ppermute(
                block, "narrow", [(at, (at + step) % n_narrow) for at in range(n_narrow)]
            )
        mod_blocks.append(block)
    mod_slot = jnp.roll(jnp.stack(mod_blocks[::-1]), narrow_index + 1, axis=0)
    modulation = mod_slot.transpose(1, 0, 2).reshape(6, width)

    packs = [own_pack]
    packs += gathered(
        [after(each, *mod_blocks[1:], token_rows[-1], *bias_packs[1:]) for each in attn_pieces]
    )
    qkv_biases = [pack[: 3 * local] for pack in bias_packs]
    up_biases = jnp.stack([pack[3 * local :] for pack in bias_packs]).reshape(slot_count, 1, -1)

    attn_in = modulated_rows(token_rows, modulation)
    qkv = [qkv_rows(attn_in, packs[0], qkv_biases[0])]

    flat_shape = (hidden_local, width)
    mlp_pack = jnp.concatenate([piece(up_weight.reshape(flat_shape)), piece(down_weight)], axis=1)
    mlp_pack = after(mlp_pack, token_rows[-1], modulation)
    mlp_pieces = fetched(mlp_pack)
    own_grad = after(out_grad, token_rows[-1], modulation)
    grad_rows = [own_grad] + [fetch_rows(own_grad, step) for step in others]

    half_rows = max(own_rows // 2, BLOCK)
    halves_of = {block: own_rows // half_rows for block in others}
    halves_of[0] = 1
    attended = [{} for _ in range(slot_count)]
    lse = [{} for _ in range(slot_count)]
    attended_turned = [{} for _ in range(slot_count)]

    def attend(index, block, half, *earlier):
        rows = own_rows // halves_of[block]
        results = attention_forward(
            after(qkv[index], *earlier), patches, block * own_rows + half * rows, rows
        )
        for kept, result in zip((attended, attended_turned, lse), results):
            kept[index][block, half] = result
        return results[0]

    parts_of = [(block, half) for block in others for half in range(halves_of[block])]
    for part in parts_of:
        last_rows = attend(0, *part)
    for index in other_shards:
        rows = after(attn_in, last_rows)
        qkv.append(qkv_rows(rows, packs[index], qkv_biases[index]))

    def branch_sum(rows, pack_refs):
        return sum(dot(each, ref[3 * local :]) for each, ref in zip(rows, pack_refs))

    zero_row = jnp.zeros((1, width), f32)
    def branch_part(part, kind):
        rows = [parts[part] for parts in attended]
        return row_call(
            lambda rows, vectors: ([branch_sum(rows, vectors[1:])], []), rows, [zero_row, *packs], [kind]
        )[0]

    arrived = {}
    earlier = []
    for part in parts_of:
        for index in other_shards:
            last_rows = attend(index, *part, *earlier)
        if not earlier:
            mlp_packs = gathered(
                [after(each, last_rows, *grad_rows[1:]) for each in mlp_pieces]
            )
        earlier = [branch_part(part, bf16)]
        arrived[part] = send_rows(earlier[0], part[0])
    last_rows = attend(0, 0, 0, *earlier)
    for index in other_shards:
        last_rows = attend(index, 0, 0, last_rows)
    own_branch = branch_part((0, 0), f32)

    def joined(parts, axis=0):
        parts = list(parts)
        return parts[0] if len(parts) == 1 else jnp.concatenate(parts, axis=axis)

    def blocks_of(parts, axis):
        return [
            joined((parts[block, half] for half in range(halves_of[block])), axis)
            for block in range(members)
        ]

    lse = [blocks_of(parts, 1) for parts in lse]
    attended_turned = [
        [parts[block, half] for block in range(members) for half in range(halves_of[block])]
        for parts in attended_turned
    ]
    arrived = [
        joined(after(arrived[block, half], own_branch) for half in range(halves_of[block]))
        for block in others
    ]

    def middle_body(rows, vectors):
        token, *rest = [each.astype(f32) for each in rows]
        mod_ref, bias_ref = vectors
        branch = sum(rest[1:], rest[0]) + bias_ref[...].astype(f32)
        normed = normalize(token + mod_ref[2:3] * branch)[0]
        return [branch, normed * (1.0 + mod_ref[4:5]) + mod_ref[3:4]], []

    branch_one, mlp_own = row_call(
        middle_body,
        [tokens, own_branch, *arrived],
        [modulation, o_bias.reshape(1, width)],
        [f32, bf16],
    )

    mlp_rows = [mlp_own] + [fetch_rows(mlp_own, step) for step in others]
    ups, downs = [(up_weight, 0)], [(down_weight, 0)]
    for pack in mlp_packs:
        if hidden_local == width and hidden_local % HIDDEN_BLOCK == 0:
            ups.append((pack, 0))
            downs.append((pack, 1))
        else:
            ups.append((pack[:, :width].reshape(up_weight.shape), 0))
            downs.append((pack[:, width:], 0))
    hidden, d_pre, d_branch_two, d_mlp, branch_two, bias_sums_up = [], [], [], [], [], []
    for block in range(members):
        rows = after(mlp_rows[block], *d_mlp)
        results = feed_forward(
            rows, grad_rows[block], modulation, up_biases, ups, downs, bf16 if block else f32
        )
        for kept, result in zip((hidden, d_pre, d_branch_two, d_mlp, branch_two, bias_sums_up), results):
            kept.append(result)
    arrived = [send_rows(d_mlp[block], block) for block in others]
    grad_mlp_part = mlp_gradients(mlp_rows, d_branch_two, hidden, d_pre, n_wide)

    def d_middle_body(rows, vectors):
        token, branch, grad, *parts = [each.astype(f32) for each in rows]
        (mod_ref,) = vectors
        d_mlp_in = sum(parts[1:], parts[0])
        normed, inverse = normalize(token + mod_ref[2:3] * branch)
        d_middle = grad + norm_back(d_mlp_in * (1.0 + mod_ref[4:5]), normed, inverse)
        d_branch_one = (mod_ref[2:3] * d_middle).astype(bf16)
        terms = [d_middle * branch, d_mlp_in, d_mlp_in * normed, d_branch_one.astype(f32)]
        return [d_branch_one, d_middle], terms

    arrived = [after(part, grad_mlp_part) for part in arrived]
    d_branch_one, d_middle, middle_sums = row_call(
        d_middle_body, [tokens, branch_one, out_grad, d_mlp[0], *arrived], [modulation], [bf16, f32], 4
    )
    mlp_scattered = lax.psum_scatter(after(grad_mlp_part, *arrived), "wide", scatter_dimension=0, tiled=True)
    d_branch_rows = [d_branch_one] + [fetch_rows(d_branch_one, step) for step in others]

    assert n_wide & (n_wide - 1) == 0
    bits = n_wide.bit_length() - 1
    chips = n_wide // 2
    core, chip = wide_index % 2, wide_index // 2

    def wide_xor(array, mask):
        return lax.ppermute(array, "wide", [(at, at ^ mask) for at in range(n_wide)])

    def start_cores(part):
        keep, send = part
        return keep, wide_xor(send, 1)

    def end_cores(started):
        return split_pieces(*started, chip)

    def start_chips(pieces):
        return [pieces[0]] + [wide_xor(each, 2 * mask) for mask, each in enumerate(pieces[1:], 1)]

    shard_order = other_shards + [0]
    d_query = [[None] * members for _ in range(slot_count)]
    d_query_turned = [[None] * members for _ in range(slot_count)]
    d_kv, d_kv_turned = [None] * slot_count, [None] * slot_count
    grad_attn_part, attn_bias_sums = [None] * slot_count, [None] * slot_count

    def attn_gradients_of(index, *earlier):
        grad_attn_part[index], attn_bias_sums[index] = attn_gradients(
            attn_in,
            after(d_kv_turned[index], *earlier),
            d_query_turned[index],
            d_branch_rows,
            attended_turned[index],
            core,
            chips,
        )

    for block in range(members):
        last = block == members - 1
        for index in shard_order:
            d_query[index][block], d_query_turned[index][block], d_kv[index], *turned = (
                attention_backward(
                    qkv[index],
                    d_branch_rows[block],
                    packs[index],
                    lse[index][block],
                    patches,
                    d_kv[index],
                    block * own_rows,
                    last,
                )
            )
            if last:
                d_kv_turned[index] = turned[0]
                if index:
                    attn_gradients_of(index)
                    d_branch_rows[block] = after(d_branch_rows[block], grad_attn_part[index][0])
        if not last:
            d_branch_rows[block + 1] = after(d_branch_rows[block + 1], d_kv[0])

    def d_attn_sum(rows, pack_refs):
        total = 0.0
        for index, ref in enumerate(pack_refs):
            total = total + dot(rows[2 * index], ref[:local])
            total = total + dot(rows[2 * index + 1], ref[local : 3 * local])
        return total

    def d_rows_of(block):
        rows = []
        for index in range(slot_count):
            rows += [d_query[index][block], (d_kv[index], block * own_rows)]
        return rows

    cores_ended = [end_cores(start_cores(part)) for part in grad_attn_part[1:]]
    chips_started_of = {index: start_chips(cores_ended[index - 1]) for index in other_shards}
    attn_gradients_of(0, *(pieces[0] for pieces in cores_ended))
    late_branch = [after(branch_two[block], *d_branch_rows[1:]) for block in others]
    arrived_two = [send_rows(part, block) for part, block in zip(late_branch, others)]
    arrived_two = [after(part, grad_attn_part[0][0]) for part in arrived_two]

    def out_body(rows, vectors):
        token, branch, grad, *parts = [each.astype(f32) for each in rows]
        mod_ref, bias_ref = vectors
        total = sum(parts[1:], parts[0]) + bias_ref[...].astype(f32)
        block_out = token + mod_ref[2:3] * branch + mod_ref[5:6] * total
        return [block_out], [grad * total, (mod_ref[5:6] * grad).astype(bf16).astype(f32)]

    block_out, out_sums = row_call(
        out_body,
        [tokens, branch_one, out_grad, branch_two[0], *arrived_two],
        [modulation, down_bias.reshape(1, width)],
        [bf16],
        2,
        FILLER_FLOPS,
    )
    mlp_scattered = after(mlp_scattered, block_out)
    mlp_sent = cut(mlp_scattered.reshape(slot_count, 2, -1, width))
    mlp_arrived = [send_shard(mlp_sent[step], step) for step in other_shards]
    d_kv[0] = after(d_kv[0], grad_attn_part[0][0], *mlp_sent[1:])
    def d_attn_part(block, kind, flops=0):
        return row_call(
            lambda rows, vectors: ([d_attn_sum(rows, vectors[1:])], []),
            d_rows_of(block),
            [zero_row, *packs],
            [kind],
            flops=flops,
        )[0]

    d_attn_parts = [d_attn_part(block, bf16) for block in others]
    arrived = [send_rows(part, block) for part, block in zip(d_attn_parts, others)]
    own_cores = start_cores(grad_attn_part[0])

    d_query[0][0] = after(d_query[0][0], *d_attn_parts)
    own_d_attn = d_attn_part(0, f32, FILLER_FLOPS)
    def end_body(rows, vectors):
        token, d_middle_rows, *parts = rows
        (mod_ref,) = vectors
        d_attn_in = sum([each.astype(f32) for each in parts[1:]], parts[0])
        normed, inverse = normalize(token.astype(f32))
        grad = d_middle_rows + norm_back(d_attn_in * (1.0 + mod_ref[1:2]), normed, inverse)
        return [grad], [d_attn_in, d_attn_in * normed]

    piece_sums = []
    for index in other_shards:
        own, *pieces = chips_started_of[index]
        piece_sums.append(add_arrays(own, *(after(each, *d_attn_parts) for each in pieces)))
    own_pieces = end_cores((own_cores[0], after(own_cores[1], *d_attn_parts)))
    own_piece_sum = add_arrays(*start_chips(own_pieces))
    arrived = [after(part, own_d_attn, own_piece_sum, *piece_sums) for part in arrived]
    grad_tokens, end_sums = row_call(
        end_body, [tokens, d_middle, own_d_attn, *arrived], [modulation], [f32], 2
    )

    sent = [send_shard(each, index) for index, each in zip(other_shards, piece_sums)]
    mlp_total = add_arrays(mlp_sent[0], *(after(each, end_sums) for each in mlp_arrived))

    middle_sums, out_sums = after(middle_sums, end_sums), after(out_sums, end_sums)
    own_sums = jnp.concatenate(
        [end_sums[0:2], middle_sums[0:3], out_sums[0:1], middle_sums[3:4], out_sums[1:2]]
    )
    bit = 1
    while bit < members:
        own_sums = own_sums + lax.ppermute(
            own_sums, "narrow", [(at, at ^ bit) for at in range(n_narrow)]
        )
        bit *= 2
    attn_bias_sums = [after(each, end_sums) for each in attn_bias_sums]
    up_bias_sums = sum([after(each, end_sums) for each in bias_sums_up])
    late_slot_clip = after(slot_clip, end_sums)
    shard_parts = [
        jnp.concatenate([attn_bias_sums[step].reshape(-1), up_bias_sums[step]])
        for step in range(slot_count)
    ]
    slot_sums = [own_sums] + [fetch_shard(own_sums, step) for step in other_shards]
    shard_parts[1:] = [send_shard(shard_parts[step], step) for step in other_shards]
    grad_mlp = lax.all_gather(mlp_total, "wide", axis=0, tiled=False)
    grad_up_weight, grad_down_weight = mlp_outputs(grad_mlp, up_weight.shape)

    clip_ids = jnp.arange(clip_count, dtype=jnp.int32)
    d_mod_clips = jnp.zeros((clip_count, 6, local), f32)
    bias_sums = jnp.zeros((2, width), f32)
    shard_sum = jnp.zeros((3 * local + hidden_local,), f32)
    for step in range(slot_count):
        source_clip = late_slot_clip[(slot + step) % slot_count]
        one_hot = (clip_ids == source_clip).astype(f32)
        columns = lax.dynamic_slice_in_dim(slot_sums[step][:6], narrow_index * local, local, 1)
        d_mod_clips = d_mod_clips + one_hot[:, None, None] * columns
        bias_sums = bias_sums + slot_sums[step][6:]
        shard_sum = shard_sum + shard_parts[step]
    small = jnp.concatenate([d_mod_clips.reshape(-1), bias_sums.reshape(-1), shard_sum])
    for bit in range(bits):
        small = small + wide_xor(small, 1 << bit)

    total = add_arrays(own_piece_sum, *(after(each, small) for each in sent))

    mod_size = clip_count * 6 * local
    d_modulation = small[:mod_size].reshape(clip_count, 6, local)
    grad_o_bias = small[mod_size : mod_size + width]
    grad_down_bias = small[mod_size + width : mod_size + 2 * width]
    shard_sum = small[mod_size + 2 * width :]
    grad_q_bias = shard_sum[:local]
    grad_v_bias = shard_sum[2 * local : 3 * local]
    grad_up_bias = shard_sum[3 * local :]

    silu_float = silu_cond.astype(f32)
    grad_ada_weight = jnp.einsum("cd,cke->dke", silu_float, d_modulation, precision=highest)
    grad_ada_bias = jnp.sum(d_modulation, axis=0)
    d_silu = jnp.einsum(
        "cke,dke->cd", d_modulation, ada_weight.astype(f32), precision=highest
    )
    far_pieces = [
        after(wide_xor(total, 2 * mask), d_silu, grad_ada_weight) for mask in range(1, chips)
    ]
    pieces = collect([total] + far_pieces, chip)
    flipped_pieces = wide_xor(pieces, 1)

    grad_q_weight, grad_k_weight, grad_v_weight, grad_o_weight = attn_outputs(
        pieces, flipped_pieces, core
    )

    bit = 1
    while bit < n_narrow:
        flipped = lax.ppermute(d_silu, "narrow", [(at, at ^ bit) for at in range(n_narrow)])
        d_silu = d_silu + (after(flipped, grad_up_weight) if bit == 1 else flipped)
        bit *= 2
    grad_condition = jax.vjp(jax.nn.silu, cond_float)[1](d_silu)[0]
    return (
        block_out,
        grad_tokens,
        grad_condition,
        grad_q_weight,
        grad_q_bias,
        grad_k_weight,
        grad_v_weight,
        grad_v_bias,
        grad_o_weight,
        grad_o_bias,
        grad_up_weight,
        grad_up_bias,
        grad_down_weight,
        grad_down_bias,
        grad_ada_weight,
        grad_ada_bias,
    )


def solution(mesh):
    in_specs = (
        P(("wide", "narrow"), None),
        P(),
        P(None, "narrow"),
        P("narrow"),
        P(None, "narrow"),
        P(None, "narrow"),
        P("narrow"),
        P("narrow", None),
        P(),
        P(None, "narrow"),
        P("narrow"),
        P("narrow", None),
        P(),
        P(None, None, "narrow"),
        P(None, "narrow"),
        P(("wide", "narrow"), None),
        P("wide"),
        P(),
    )
    out_specs = (
        P(("wide", "narrow"), None),
        P(("wide", "narrow"), None),
        P(),
        P(None, "narrow"),
        P("narrow"),
        P(None, "narrow"),
        P(None, "narrow"),
        P("narrow"),
        P("narrow", None),
        P(),
        P(None, "narrow"),
        P("narrow"),
        P("narrow", None),
        P(),
        P(None, None, "narrow"),
        P(None, "narrow"),
    )
    return jax.shard_map(shards, mesh=mesh, in_specs=in_specs, out_specs=out_specs, check_vma=False)
```
